32 devices in a mesh: row: 8 (over y, x, core), col: 4 (over z).
Axes of the slice: x: 2, y: 2, z: 4, core: 2. Of those that a mesh axis runs over, the one named last changes fastest.
Arguments:
- images: bfloat16 [4, 4, 16, 3072], P(None, 'col', 'row'), may hold values from -6 to 6
- cotangent: bfloat16 [16, 16, 4, 4, 16], P('row', None, None, 'col'), may hold values from -192 to 192
Outputs:
- kernel: float32 [16, 16, 4, 4, 16], P('row', None, None, 'col')
- image_grads: float32 [4, 4, 16, 3072], P(None, 'col', 'row')
The draws below stay inside these ranges and needn't reach their ends.
All inputs are finite; a program needn't handle non-finite values.
Results may differ from the reference program's by a relative error of at most 0.0003.
Values may be sent and summed in bfloat16 or wider, within the bound.
No kernel may reach another device: no remote copies, remote signals or barrier semaphores. Data moves between devices by JAX's collectives and lax.ppermute only.
A program may use at most 64 MiB of HBM per device.

```python
import math
import jax
import jax.numpy as jnp
import numpy as np
from jax import lax

CHAN = 3
TILE = 16
LAYERS = 3
FEAT = 3072
NBLK = 16
KB = 4
N_ROW = 8
N_COL = 4


def block_levels(own_key, shape, pieces, smallest, high):
    def one(dim, blocks):
        heights = jax.random.uniform(jax.random.fold_in(jax.random.fold_in(own_key, 6), dim), (blocks,), jnp.float32, smallest / len(pieces), high / len(pieces))
        return jnp.repeat(jnp.exp(heights), shape[dim] // blocks).reshape((-1,) + (1,) * (len(shape) - dim - 1))

    level = one(*pieces[0])
    for cut in pieces[1:]:
        level = level * one(*cut)
    return level


def scatter_about(rng, dims, spread, limit, split=(), kind=jnp.bfloat16):
    values = spread * jax.random.normal(rng, dims, jnp.float32)
    if split:
        values = values * block_levels(rng, dims, split, -0.22, 0.18)
    return jnp.clip(values, -limit, limit).astype(kind)


def setup_inputs(seed: int = 0) -> dict:
    splits = jax.random.split(jax.random.key(seed), 3)
    images = scatter_about(splits[0], (KB, N_COL, TILE, FEAT), 1.0, 6.0, ((1, 4), (2, 8)))
    cotangent = scatter_about(splits[1], (NBLK, TILE, KB, N_COL, TILE), 32.0, 192.0, ((0, 8), (3, 4)))
    return {"images": images, "cotangent": cotangent}


WEIGHT_VAR = 2.0
BIAS_VAR = 0.1

def shifted(field, offset):
    total = field.shape[-1]
    widths = [(0, 0)] * (field.ndim - 1) + [(max(-offset, 0), max(offset, 0))]
    padded = jnp.pad(field, widths)
    begin = max(offset, 0)
    return padded[..., begin:begin + total]

def spatial_blur(field, grid_side):
    column = jnp.arange(grid_side * grid_side) % grid_side
    left_ok = (column > 0).astype(jnp.float32)
    right_ok = (column < grid_side - 1).astype(jnp.float32)
    across = field + shifted(field, -1) * left_ok + shifted(field, 1) * right_ok
    summed = across + shifted(across, -grid_side) + shifted(across, grid_side)
    return WEIGHT_VAR * summed / 9.0 + BIAS_VAR

def relu_expect(cross_cov, left_var, right_var):
    fixed_cross = lax.stop_gradient(cross_cov)
    fixed_left = lax.stop_gradient(left_var)
    fixed_right = lax.stop_gradient(right_var)
    root_prod = jnp.sqrt(fixed_left * fixed_right)
    cosine = jnp.clip(fixed_cross / root_prod, -1.0, 1.0)
    angle_val = jnp.arccos(cosine)
    sine_val = jnp.sqrt(jnp.maximum(1.0 - cosine * cosine, 0.0))
    value = root_prod * (sine_val + (jnp.pi - angle_val) * cosine) / (2.0 * jnp.pi)
    slope_cross = (jnp.pi - angle_val) / (2.0 * jnp.pi)
    slope_left = jnp.sqrt(fixed_right / fixed_left) * sine_val / (4.0 * jnp.pi)
    slope_right = jnp.sqrt(fixed_left / fixed_right) * sine_val / (4.0 * jnp.pi)
    linear = slope_cross * cross_cov + slope_left * left_var + slope_right * right_var
    return lax.stop_gradient(value - linear) + linear

def tile_kernel(left_imgs, right_imgs):
    tile_rows = left_imgs.shape[0]
    positions = left_imgs.shape[1] // CHAN
    grid_side = math.isqrt(positions)
    left_px = left_imgs.reshape(tile_rows, CHAN, positions)
    right_px = right_imgs.reshape(right_imgs.shape[0], CHAN, positions)
    cross_cov = jnp.einsum('acp,bcp->abp', left_px, right_px, precision=lax.Precision.HIGHEST) / CHAN
    left_var = lax.optimization_barrier(jnp.sum(left_px * left_px, axis=1)) / CHAN
    right_var = lax.optimization_barrier(jnp.sum(right_px * right_px, axis=1)) / CHAN
    for layer_idx in range(LAYERS):
        cross_cov = spatial_blur(cross_cov, grid_side)
        left_var = spatial_blur(left_var, grid_side)
        right_var = spatial_blur(right_var, grid_side)
        cross_cov = relu_expect(cross_cov, left_var[:, None, :], right_var[None, :, :])
        left_var = 0.5 * left_var
        right_var = 0.5 * right_var
    return WEIGHT_VAR * lax.optimization_barrier(jnp.mean(cross_cov, axis=-1)) + BIAS_VAR

def tile_terms(left_blk, right_blk, cot_blk):
    left_full = left_blk.astype(jnp.float32)
    right_full = right_blk.astype(jnp.float32)
    value, pullback = jax.vjp(tile_kernel, left_full, right_full)
    grad_left, grad_right = pullback(cot_blk.astype(jnp.float32))
    return (value, grad_left, grad_right)

def reference(images, cotangent):
    block_count = 2 * N_ROW
    blocks = images.reshape(block_count, TILE, FEAT)
    cot_grid = cotangent.reshape(block_count, TILE, block_count, TILE)
    table = np.array([(first, second) for first in range(block_count) for second in range(first, block_count)], dtype=np.int32)
    zero_idx = jnp.zeros((), jnp.int32)

    def step_fn(carry, pair_ids):
        grads, kernel = carry
        first = pair_ids[0].astype(jnp.int32)
        second = pair_ids[1].astype(jnp.int32)
        left_blk = lax.dynamic_index_in_dim(blocks, first, 0, keepdims=False)
        right_blk = lax.dynamic_index_in_dim(blocks, second, 0, keepdims=False)
        cot_blk = lax.dynamic_slice(cot_grid, (first, zero_idx, second, zero_idx), (1, TILE, 1, TILE)).reshape(TILE, TILE)
        value, grad_left, grad_right = tile_terms(left_blk, right_blk, cot_blk)
        grads = grads.at[first].add(grad_left)
        grads = grads.at[second].add(grad_right)
        kernel = lax.dynamic_update_slice(kernel, value.reshape(1, TILE, 1, TILE), (first, zero_idx, second, zero_idx))
        return ((grads, kernel), None)
    start = (jnp.zeros((block_count, TILE, FEAT), jnp.float32), jnp.zeros((block_count, TILE, block_count, TILE), jnp.float32))
    (grads, kernel), unused = lax.scan(step_fn, start, jnp.asarray(table))
    return (kernel.reshape(block_count, TILE, KB, N_COL, TILE), grads.reshape(KB, N_COL, TILE, FEAT))
```

```python
import functools, math
import jax, jax.numpy as jnp, numpy as np
from jax import lax
from jax.experimental import pallas as pl
from jax.experimental.pallas import tpu as pltpu
from jax.sharding import PartitionSpec as P

CHAN = 3
LAYERS = 3
WEIGHT_VAR = 2.0
BIAS_VAR = 0.1
LANES = 128
SUBS = 8
TINY = 1e-30
F32 = jnp.float32


def arccos_coefficients(degree):
    nodes = 0.5 + 0.5 * np.cos(np.pi * (np.arange(400) + 0.5) / 400)
    target = np.arccos(1.0 - nodes) / np.sqrt(nodes)
    fit = np.polynomial.chebyshev.Chebyshev.fit(nodes, target, degree, domain=[0.0, 1.0])
    return [float(c) for c in fit.convert(kind=np.polynomial.Polynomial).coef]


COEFFS = arccos_coefficients(6)


def row_sums(ref, v, cols):
    f = [ref[j, v] for j in range(cols)]
    sub = lax.broadcasted_iota(jnp.int32, (SUBS, LANES), 0)
    above = jnp.where(sub > 0, pltpu.roll(f[-1], 1, 0), 0.0)
    below = jnp.where(sub < SUBS - 1, pltpu.roll(f[0], SUBS - 1, 0), 0.0)
    g = [above] + f + [below]
    out = []
    for j in range(0, cols, 2):
        mid = g[j + 1] + g[j + 2]
        out.append(g[j] + mid)
        out.append(mid + g[j + 3])
    return out


def sweep(ref, side, cols, emit, carry=(), chunk=8):
    def body(i, state):
        prev, cur, extra = state
        base = i * chunk
        for o in range(0, chunk, 2):
            nxt = row_sums(ref, base + o + 2, cols)
            nxt2 = row_sums(ref, base + o + 3, cols)
            mid = [a + b for a, b in zip(cur, nxt)]
            extra = emit(base + o, [a + b for a, b in zip(prev, mid)], extra)
            extra = emit(base + o + 1, [a + b for a, b in zip(mid, nxt2)], extra)
            prev, cur = nxt, nxt2
        return prev, cur, extra

    zero = [jnp.zeros((SUBS, LANES), F32) for _ in range(cols)]
    first = row_sums(ref, 1, cols)
    return lax.fori_loop(0, side // chunk, body, (zero, first, carry))[2]


def one_hot(index, count):
    return (lax.broadcasted_iota(jnp.int32, (index.shape[0], count), 1) == index).astype(F32)


def reversed_bits(x, count):
    out = 0 * x
    bit = 1
    while bit < count:
        out = 2 * out + x // bit % 2
        bit *= 2
    return out


def exact_dot(a, b, dims):
    return lax.dot_general(a, b, (dims, ((), ())), precision=lax.Precision.HIGHEST,
                           preferred_element_type=F32)


def kernel_body(dims, mode_ref, xa_ref, xb_ref, ca_ref, cb_ref, pa_ref, pb_ref, ga_ref, gb_ref,
                t_ref, y_ref, xr_ref, v_ref, sg_ref, f_ref, phi_ref, sin_ref, d_ref, g_ref, w_ref, kv_ref):
    gs, npos, side, col_count, per_row, part = dims
    members = gs // (per_row * part)
    tile_rows = 2 * members * part
    rows_of_dev = 2 * tile_rows
    width = per_row * tile_rows
    two = 2 * gs
    cols = side // SUBS
    tiles = gs * gs // LANES
    apt = LANES // gs
    blocks = npos // LANES
    bts = gs // SUBS
    per = LANES // SUBS
    diag = mode_ref[0] == 1
    member = mode_ref[1]
    lane = lax.broadcasted_iota(jnp.int32, (SUBS, LANES), 1)

    def col_of(tile):
        return tile // side, tile % side + 1

    def places(col, half, axis):
        shape = (gs, 1) if axis == 0 else (1, gs)
        i = lax.broadcasted_iota(jnp.int32, shape, axis)
        k = i // part % per_row
        held = jnp.bitwise_xor(member, reversed_bits(i // (part * per_row), members))
        idx = (half * members + held) * part + i % part
        blk = k * col_count + col
        return blk, blk * tile_rows + idx, k * tile_rows + idx
    col_a, half_a, col_b, half_b = mode_ref[2], mode_ref[3], mode_ref[4], mode_ref[5]
    blk_a, row_a, at_a = places(col_a, half_a, 0)
    blk_b, row_b, at_b = places(col_b, half_b, 0)
    blk_al = places(col_a, half_a, 1)[0]
    blk_bl = places(col_b, half_b, 1)[0]
    total_rows = ca_ref.shape[0]
    eye = (lax.broadcasted_iota(jnp.int32, (gs, gs), 0) == lax.broadcasted_iota(jnp.int32, (gs, gs), 1))
    upper = (lax.broadcasted_iota(jnp.int32, (gs, gs), 0) < lax.broadcasted_iota(jnp.int32, (gs, gs), 1))
    row_hot_a, row_hot_b = one_hot(row_a, total_rows), one_hot(row_b, total_rows)
    col_hot_a, col_hot_b = one_hot(at_a, width), one_hot(at_b, width)
    keep_ab = (blk_a <= blk_bl).astype(F32)
    keep_ba = (blk_b <= blk_al).astype(F32)
    keep_aa = (blk_a <= blk_al).astype(F32)
    keep_bb = (blk_b <= blk_bl).astype(F32)

    def chosen(rows, table, columns):
        picked = jnp.dot(rows.astype(jnp.bfloat16), table, preferred_element_type=F32)
        return lax.dot_general(picked.astype(jnp.bfloat16), columns.astype(jnp.bfloat16),
                               (((1,), (1,)), ((), ())), preferred_element_type=F32)
    ca, cb = ca_ref[...], cb_ref[...]
    w_ab = chosen(row_hot_a, cb, col_hot_b) * keep_ab
    w_ba = chosen(row_hot_b, ca, col_hot_a) * keep_ba
    w_aa = chosen(row_hot_a, ca, col_hot_a) * keep_aa
    w_bb = chosen(row_hot_b, cb, col_hot_b) * keep_bb
    w_off = w_ab + w_ba.T
    w_diag = jnp.where(eye, 0.0, jnp.where(upper, w_aa + w_aa.T, w_bb + w_bb.T))
    w_all = jnp.where(diag, w_diag, w_off)
    hot_rows = lax.broadcasted_iota(jnp.int32, (tiles, gs), 0) * apt
    hot_cols = lax.broadcasted_iota(jnp.int32, (tiles, gs), 1)
    w_rows = jnp.concatenate(
        [exact_dot((hot_cols == hot_rows + i).astype(F32), w_all, ((1,), (0,))) for i in range(apt)], 1)
    for k in range(tiles):
        w_ref[k] = w_rows[k:k + 1]
    self_a = jnp.sum(jnp.where(eye, w_aa, 0.0), 0, keepdims=True)
    self_b = jnp.sum(jnp.where(eye, w_bb, 0.0), 0, keepdims=True)
    self_row = jnp.concatenate([jnp.zeros((1, two), F32), self_a, self_b], 1)
    self_row = jnp.where(diag, self_row, 0.0)

    for s in range(blocks):
        for h in range(2):
            parts = []
            for ch in (2 * h, 2 * h + 1):
                if ch < CHAN:
                    sl = pl.ds(ch * npos + s * LANES, LANES)
                    parts += [xa_ref[:, sl].astype(F32), xb_ref[:, sl].astype(F32)]
                else:
                    for ref in (xa_ref, xb_ref):
                        total = 0.0
                        for c in range(CHAN):
                            x = ref[:, pl.ds(c * npos + s * LANES, LANES)].astype(F32)
                            total = total + x * x
                        parts.append(total * (1.0 / CHAN))
            t_ref[h, pl.ds(s * LANES, LANES), :] = jnp.concatenate(parts, 0).T
    zeros = jnp.zeros((SUBS, LANES), F32)
    for j in range(cols):
        for v in (0, side + 1):
            f_ref[0, j, v] = zeros
            f_ref[1, j, v] = zeros
            y_ref[0, j, v] = zeros
            y_ref[1, j, v] = zeros
            for l in range(LAYERS):
                v_ref[l, j, v] = zeros
                phi_ref[l, j, v] = zeros
    def regroup(v, _):
        for j in range(cols):
            for h in range(2):
                y_ref[h, j, v + 1] = t_ref[h, pl.ds(j * side + v, SUBS, stride=LANES), :]
        return 0
    lax.fori_loop(0, side, regroup, 0)

    def block_of(ref_at, blk):
        vals = []
        for t in range(per):
            j, v = col_of(blk * per + t)
            vals.append(ref_at(j, v))
        return jnp.concatenate(vals, 0)

    for blk in range(blocks):
        for h in range(2):
            xr_ref[h, :, pl.ds(blk * LANES, LANES)] = block_of(lambda j, v: y_ref[h, j, v], blk).T
    def var_emit(l, scale):
        def emit(v, sums, extra):
            for j in range(cols):
                v_ref[l, j, v + 1] = sums[j] * scale + BIAS_VAR
            return extra
        return emit
    sweep(y_ref.at[1], side, cols, var_emit(0, WEIGHT_VAR / 9.0))
    sweep(v_ref.at[0], side, cols, var_emit(1, 0.5 * WEIGHT_VAR / 9.0))
    sweep(v_ref.at[1], side, cols, var_emit(2, 0.5 * WEIGHT_VAR / 9.0))
    for l in range(LAYERS):
        for blk in range(blocks):
            t = block_of(lambda j, v: v_ref[l, j, v], blk).T
            t = t[two:]
            sg_ref[l, :, pl.ds(blk * LANES, LANES)] = t * lax.rsqrt(t)
    total = jnp.zeros((SUBS, LANES), F32)
    for j in range(cols):
        for v in range(side):
            total = total + v_ref[LAYERS - 1, j, v + 1]
    kself = jnp.sum(total, 0, keepdims=True) * (0.5 * WEIGHT_VAR / npos) + BIAS_VAR

    def zero_acc(i, _):
        sl = pl.ds(pl.multiple_of(i * LANES, LANES), LANES)
        for l in range(LAYERS):
            d_ref[l, :, sl] = jnp.zeros((2 * two, LANES), F32)
        for h in range(2):
            g_ref[h, :, sl] = jnp.zeros((LANES, LANES), F32)
        return 0
    lax.fori_loop(0, blocks, zero_acc, 0)

    sub = lax.broadcasted_iota(jnp.int32, (SUBS, LANES), 0)

    def rows_of(ref, slot, base, k, sl):
        at = pl.multiple_of(base + k * apt // SUBS * SUBS, SUBS)
        t = pltpu.roll(ref[slot, pl.ds(at, SUBS), sl], (SUBS - k * apt % SUBS) % SUBS, 0)
        return [t[a:a + 1] for a in range(apt)]

    def add_rows(ref, slot, base, k, sl, rows):
        at = pl.multiple_of(base + k * apt // SUBS * SUBS, SUBS)
        t = jnp.concatenate(rows + [jnp.zeros((SUBS - apt, LANES), F32)], 0)
        ref[slot, pl.ds(at, SUBS), sl] = ref[slot, pl.ds(at, SUBS), sl] + pltpu.roll(t, k * apt % SUBS, 0)

    def xtile(ch, img, sl):
        return xr_ref[ch // 2, pl.ds((ch % 2) * two + img, SUBS), sl]

    def pair_tile(k, _):
        a0 = k * apt

        def cross_plain(blk, _):
            sl = pl.ds(pl.multiple_of(blk * LANES, LANES), LANES)
            rows = []
            lefts = [rows_of(xr_ref, ch // 2, (ch % 2) * two, k, sl) for ch in range(CHAN)]
            for a in range(apt):
                left = [lefts[ch][a] for ch in range(CHAN)]
                for bt in range(bts):
                    acc = left[0] * xtile(0, gs + bt * SUBS, sl)
                    for ch in range(1, CHAN):
                        acc = acc + left[ch] * xtile(ch, gs + bt * SUBS, sl)
                    rows.append(acc)
            put(blk, jnp.concatenate(rows, 0).T)
            return 0

        def cross_diag(blk, _):
            sl = pl.ds(pl.multiple_of(blk * LANES, LANES), LANES)
            rows = []
            lefts = [[rows_of(xr_ref, ch // 2, (ch % 2) * two + o, k, sl) for ch in range(CHAN)]
                     for o in (0, gs)]
            for a in range(apt):
                l0 = [lefts[0][ch][a] for ch in range(CHAN)]
                l1 = [lefts[1][ch][a] for ch in range(CHAN)]
                for bt in range(bts):
                    first = sub + bt * SUBS > a0 + a
                    acc = 0.0
                    for ch in range(CHAN):
                        acc = acc + jnp.where(first, l0[ch], l1[ch]) * jnp.where(
                            first, xtile(ch, bt * SUBS, sl), xtile(ch, gs + bt * SUBS, sl))
                    rows.append(acc)
            put(blk, jnp.concatenate(rows, 0).T)
            return 0

        def put(blk, t):
            half = blk * per
            j = half // side
            v = half % side + 1
            for i in range(per):
                f_ref[0, j, v + i] = t[i * SUBS:(i + 1) * SUBS]

        @pl.when(jnp.logical_not(diag))
        def _():
            lax.fori_loop(0, blocks, cross_plain, 0)

        @pl.when(diag)
        def _():
            lax.fori_loop(0, blocks, cross_diag, 0)

        ia = a0 + lane // gs
        ib = lane % gs
        second = jnp.logical_and(diag, ib <= ia)
        il = two + ia + jnp.where(second, gs, 0)
        ir = two + ib + jnp.where(jnp.logical_and(diag, ib > ia), 0, gs)

        def relu_emit(l, scale, dst):
            def emit(v, sums, extra):
                for j in range(cols):
                    k12 = sums[j] * scale + BIAS_VAR
                    var = v_ref[l, j, v + 1]
                    prod = jnp.take_along_axis(var, il, axis=1) * jnp.take_along_axis(var, ir, axis=1)
                    inv = lax.rsqrt(prod)
                    cosine = k12 * inv
                    w = jnp.maximum(1.0 - jnp.abs(cosine), TINY)
                    poly = COEFFS[-1]
                    for c in COEFFS[-2::-1]:
                        poly = poly * w + c
                    angle = (w * lax.rsqrt(w)) * poly
                    phi = jnp.where(cosine >= 0.0, math.pi - angle, angle)
                    rest = jnp.maximum(prod - k12 * k12, TINY)
                    root = rest * lax.rsqrt(rest)
                    value = root + phi * k12
                    phi_ref[l, j, v + 1] = phi
                    sin_ref[l, j, v + 1] = root * inv
                    if dst is None:
                        extra = extra + value
                    else:
                        f_ref[dst, j, v + 1] = value
                return extra
            return emit

        inner = WEIGHT_VAR / (9.0 * 2.0 * math.pi)
        sweep(f_ref.at[0], side, cols, relu_emit(0, WEIGHT_VAR / (9.0 * CHAN), 1))
        sweep(f_ref.at[1], side, cols, relu_emit(1, inner, 0))
        total = sweep(f_ref.at[0], side, cols, relu_emit(2, inner, None), jnp.zeros((SUBS, LANES), F32))
        kv_ref[k] = jnp.sum(total, 0, keepdims=True) * (
            WEIGHT_VAR / (2.0 * math.pi * npos)) + BIAS_VAR

        wrow = w_ref[k] * (WEIGHT_VAR / npos)
        wrow = jnp.broadcast_to(wrow, (SUBS, LANES))
        wscaled = wrow * inner

        def back_emit(l, dst, scaled):
            def emit(v, sums, extra):
                for j in range(cols):
                    grad = sums[j] * wscaled if scaled else sums[j]
                    sin_ref[l, j, v + 1] = sin_ref[l, j, v + 1] * grad
                    f_ref[dst, j, v + 1] = phi_ref[l, j, v + 1] * grad
                return extra
            return emit
        sweep(phi_ref.at[2], side, cols, back_emit(1, 0, True))
        sweep(f_ref.at[0], side, cols, back_emit(0, 1, False))

        def last_emit(v, sums, extra):
            for j in range(cols):
                f_ref[0, j, v + 1] = sums[j]
            return extra
        sweep(f_ref.at[1], side, cols, last_emit)

        def fold(is_diag):
            def body(blk, _):
                sl = pl.ds(pl.multiple_of(blk * LANES, LANES), LANES)
                half = blk * per
                j = half // side
                v = half % side + 1

                def turned(get):
                    return jnp.concatenate([get(j, v + i) for i in range(per)], 0).T

                for l in range(LAYERS + 1):
                    if l < LAYERS - 1:
                        h = turned(lambda j, v: sin_ref[l, j, v])
                    elif l == LAYERS - 1:
                        h = turned(lambda j, v: sin_ref[l, j, v] * wrow)
                    else:
                        h = turned(lambda j, v: f_ref[0, j, v])
                    h = [[h[(a * bts + bt) * SUBS:(a * bts + bt + 1) * SUBS] for bt in range(bts)]
                         for a in range(apt)]
                    if l < LAYERS:
                        terms = [(d_ref, l, two, sg_ref, l, 0)]
                    else:
                        terms = [(g_ref, ch // 2, (ch % 2) * two, xr_ref, ch // 2, (ch % 2) * two)
                                 for ch in range(CHAN)]
                    for acc, slot, base, src, at0, base0 in terms:
                        if not is_diag:
                            left = rows_of(src, at0, base0, k, sl)
                            sums = [0.0] * apt
                            for bt in range(bts):
                                right = src[at0, pl.ds(base0 + gs + bt * SUBS, SUBS), sl]
                                out = 0.0
                                for a in range(apt):
                                    out = out + h[a][bt] * left[a]
                                    sums[a] = sums[a] + h[a][bt] * right
                                at = pl.ds(base + gs + bt * SUBS, SUBS)
                                acc[slot, at, sl] = acc[slot, at, sl] + out
                            add_rows(acc, slot, base, k, sl, [jnp.sum(t, 0, keepdims=True) for t in sums])
                        else:
                            for side_set in range(2):
                                off = side_set * gs
                                left = rows_of(src, at0, base0 + off, k, sl)
                                sums = [0.0] * apt
                                for bt in range(bts):
                                    right = src[at0, pl.ds(base0 + off + bt * SUBS, SUBS), sl]
                                    out = 0.0
                                    for a in range(apt):
                                        row = sub + bt * SUBS
                                        keep = row < a0 + a if side_set else row > a0 + a
                                        part = jnp.where(keep, h[a][bt], 0.0)
                                        out = out + part * left[a]
                                        sums[a] = sums[a] + part * right
                                    at = pl.ds(base + off + bt * SUBS, SUBS)
                                    acc[slot, at, sl] = acc[slot, at, sl] + out
                                add_rows(acc, slot, base + off, k, sl, [jnp.sum(t, 0, keepdims=True) for t in sums])
                return 0
            lax.fori_loop(0, blocks, body, 0)

        @pl.when(jnp.logical_not(diag))
        def _():
            fold(False)

        @pl.when(diag)
        def _():
            fold(True)
        return 0

    lax.fori_loop(0, tiles, pair_tile, 0)

    step = WEIGHT_VAR / (9.0 * 2.0 * math.pi)
    for l in range(LAYERS):
        for blk in range(blocks):
            t = d_ref[l, :, pl.ds(blk * LANES, LANES)].T
            for i in range(per):
                j, v = col_of(blk * per + i)
                scale = (1.0 if l == 2 else 1.0 if l == 1 else step) / (4.0 * math.pi)
                sin_ref[l, j, v] = t[i * SUBS:(i + 1) * SUBS] * lax.rsqrt(v_ref[l, j, v]) * scale
    selfw = self_row * (0.5 * WEIGHT_VAR / npos)
    def seed(v, _):
        for j in range(cols):
            phi_ref[2, j, v + 1] = sin_ref[2, j, v + 1] + selfw
        return 0
    lax.fori_loop(0, side, seed, 0)
    def chain_emit(l):
        def emit(v, sums, extra):
            for j in range(cols):
                phi_ref[l, j, v + 1] = sin_ref[l, j, v + 1] + sums[j] * (0.5 * WEIGHT_VAR / 9.0)
            return extra
        return emit
    sweep(phi_ref.at[2], side, cols, chain_emit(1))
    sweep(phi_ref.at[1], side, cols, chain_emit(0))
    for h in range(2):
        for blk in range(blocks):
            t = g_ref[h, :, pl.ds(blk * LANES, LANES)].T
            for i in range(per):
                j, v = col_of(blk * per + i)
                f_ref[h, j, v] = t[i * SUBS:(i + 1) * SUBS]
    low = lane < two
    def final_emit(v, sums, extra):
        for j in range(cols):
            e = sums[j] * (WEIGHT_VAR / 9.0 * 2.0 / CHAN)
            e = jnp.where(low, pltpu.roll(e, two, 1), e)
            for h in range(2):
                t_ref[h, pl.ds(j * side + v, SUBS, stride=LANES), :] = (
                    f_ref[h, j, v + 1] * (step * step / CHAN) + y_ref[h, j, v + 1] * e)
        return extra
    sweep(phi_ref.at[0], side, cols, final_emit)
    for h in range(2):
        for s in range(blocks):
            t = t_ref[h, pl.ds(s * LANES, LANES), :].T
            for q in range(2):
                ch = 2 * h + q
                if ch < CHAN:
                    sl = pl.ds(ch * npos + s * LANES, LANES)
                    ga_ref[:, sl] = t[q * two:q * two + gs]
                    gb_ref[:, sl] = t[q * two + gs:(q + 1) * two]

    kv = jnp.concatenate([kv_ref[k] for k in range(tiles)], 0)
    values = 0.0
    for i in range(apt):
        values = values + exact_dot((hot_cols == hot_rows + i).astype(F32), kv[:, i * gs:(i + 1) * gs],
                                    ((0,), (0,)))
    self_va = jnp.where(eye, kself[:, two:two + gs], 0.0)
    self_vb = jnp.where(eye, kself[:, two + gs:], 0.0)
    up = jnp.where(upper, values, 0.0)
    lo = jnp.where(jnp.logical_or(upper, eye), 0.0, values)
    val_aa = (up + up.T + self_va) * keep_aa
    val_bb = (lo + lo.T + self_vb) * keep_bb
    def place(at_row, device):
        ahead = reversed_bits(jnp.bitwise_xor(at_row // rows_of_dev, device), total_rows // rows_of_dev)
        return ahead * rows_of_dev + at_row % rows_of_dev

    def spread(rows, vals, columns):
        return exact_dot(one_hot(rows, total_rows), exact_dot(vals, columns, ((1,), (0,))), ((0,), (0,)))
    rows_here = place(jnp.where(diag, row_a, row_b), mode_ref[6])
    pa_ref[...] = spread(rows_here, jnp.where(diag, val_aa, values.T * keep_ba), col_hot_a)
    rows_there = place(jnp.where(diag, row_b, row_a), mode_ref[7])
    pb_ref[...] = spread(rows_there, jnp.where(diag, val_bb, values * keep_ab), col_hot_b)


def pair_kernel(mode, xa, xb, ca, cb, col_count, per_row, part):
    gs, feat = xa.shape
    npos = feat // CHAN
    side = math.isqrt(npos)
    cols = side // SUBS
    tiles = gs * gs // LANES
    dims = (gs, npos, side, col_count, per_row, part)
    field = (cols, side + 2, SUBS, LANES)
    vm = pl.BlockSpec(memory_space=pltpu.VMEM)
    return pl.pallas_call(
        functools.partial(kernel_body, dims),
        out_shape=(jax.ShapeDtypeStruct(ca.shape, F32),
                   jax.ShapeDtypeStruct(cb.shape, F32),
                   jax.ShapeDtypeStruct((gs, feat), F32),
                   jax.ShapeDtypeStruct((gs, feat), F32)),
        in_specs=[pl.BlockSpec(memory_space=pltpu.SMEM), vm, vm, vm, vm],
        out_specs=(vm, vm, vm, vm),
        scratch_shapes=[
            pltpu.VMEM((2, npos, LANES), F32),
            pltpu.VMEM((2,) + field, F32),
            pltpu.VMEM((2, LANES, npos), F32),
            pltpu.VMEM((LAYERS,) + field, F32),
            pltpu.VMEM((LAYERS, 2 * gs, npos), F32),
            pltpu.VMEM((2,) + field, F32),
            pltpu.VMEM((LAYERS,) + field, F32),
            pltpu.VMEM((LAYERS,) + field, F32),
            pltpu.VMEM((LAYERS, 4 * gs, npos), F32),
            pltpu.VMEM((2, LANES, npos), F32),
            pltpu.VMEM((tiles, 1, LANES), F32),
            pltpu.VMEM((tiles, 1, LANES), F32),
        ],
        compiler_params=pltpu.CompilerParams(vmem_limit_bytes=48 * 1024 * 1024),
        cost_estimate=pl.CostEstimate(flops=2 * 10**8, bytes_accessed=2 * 10**6, transcendentals=10**6),
        name="pair_fields",
    )(mode, xa, xb, ca, cb)


def exchange(x, rows, cols, target):
    perm = []
    for r in range(rows):
        for c in range(cols):
            tr, tc = target(r, c)
            perm.append((r * cols + c, tr * cols + tc))
    return lax.ppermute(x, ("row", "col"), perm)


def body(images, cotangent):
    rows = lax.axis_size("row")
    cols = lax.axis_size("col")
    row = lax.axis_index("row")
    col = lax.axis_index("col")
    per_row, _, part, feat = images.shape
    members = rows // 2
    groups = 2 * cols
    assert members == cols and members & (members - 1) == 0
    tile_rows = part * rows
    own = images.reshape(per_row * part, feat)

    def partner_of(r, c):
        half, m = r // members, r % members
        other = (half * cols + c + 1 + m) % groups
        return other // cols * members + m, other % cols

    def holder_of(r, c):
        half, m = r // members, r % members
        other = (half * cols + c - 1 - m) % groups
        return other // cols * members + m, other % cols

    cot_col = lax.all_gather(cotangent.reshape(2 * tile_rows, per_row * tile_rows), "row", axis=0, tiled=True)
    mine = own
    step = members // 2
    while step:
        s = step
        mine = jnp.concatenate([mine, exchange(mine, rows, cols, lambda r, c: (r ^ s, c))], 0)
        step //= 2
    theirs = exchange(mine, rows, cols, holder_of)
    cot_theirs = exchange(cot_col, rows, cols, holder_of)
    p_row, p_col = partner_of(row, col)
    member = row % members
    half = row // members
    diag = jnp.logical_and(member == members - 1, half == 1)
    mode = jnp.stack([diag.astype(jnp.int32), member, col, half, p_col, p_row // members, row, p_row])
    mode = mode.astype(jnp.int32)
    pa, pb, ga, gb = pair_kernel(mode, mine, theirs, cot_col, cot_theirs, cols, per_row, part)
    grads = ga + exchange(gb, rows, cols, partner_of)
    table = pa + exchange(pb, rows, cols, partner_of)
    step = 1
    while step < rows:
        s = step
        n = table.shape[0] // 2
        table = table[:n] + exchange(table[n:], rows, cols, lambda r, c: (r ^ s, c))
        if s < members:
            n = grads.shape[0] // 2
            grads = grads[:n] + exchange(grads[n:], rows, cols, lambda r, c: (r ^ s, c))
        step *= 2
    return (table.reshape(2, tile_rows, per_row, 1, tile_rows),
            grads.reshape(per_row, 1, part, feat))


def solution(mesh):
    return jax.shard_map(
        body,
        mesh=mesh,
        in_specs=(P(None, "col", "row", None), P("row", None, None, "col", None)),
        out_specs=(P("row", None, None, "col", None), P(None, "col", "row", None)),
        check_vma=False,
    )
```

```python
import functools, math
import jax, jax.numpy as jnp, numpy as np
from jax import lax
from jax.experimental import pallas as pl
from jax.experimental.pallas import tpu as pltpu
from jax.sharding import PartitionSpec as P

CHAN = 3
LAYERS = 3
WEIGHT_VAR = 2.0
BIAS_VAR = 0.1
LANES = 128
SUBS = 8
TINY = 1e-30
F32 = jnp.float32


def arccos_coefficients(degree):
    nodes = 0.5 + 0.5 * np.cos(np.pi * (np.arange(400) + 0.5) / 400)
    target = np.arccos(1.0 - nodes) / np.sqrt(nodes)
    fit = np.polynomial.chebyshev.Chebyshev.fit(nodes, target, degree, domain=[0.0, 1.0])
    return [float(c) for c in fit.convert(kind=np.polynomial.Polynomial).coef]


COEFFS = arccos_coefficients(5)


def row_sums(ref, v, cols):
    f = [ref[j, v] for j in range(cols)]
    sub = lax.broadcasted_iota(jnp.int32, (SUBS, LANES), 0)
    above = jnp.where(sub > 0, pltpu.roll(f[-1], 1, 0), 0.0)
    below = jnp.where(sub < SUBS - 1, pltpu.roll(f[0], SUBS - 1, 0), 0.0)
    g = [above] + f + [below]
    out = []
    for j in range(0, cols, 2):
        mid = g[j + 1] + g[j + 2]
        out.append(g[j] + mid)
        out.append(mid + g[j + 3])
    return out


def sweep(ref, side, cols, emit, carry=(), chunk=32):
    def body(i, state):
        prev, cur, extra = state
        base = i * chunk
        for o in range(0, chunk, 2):
            nxt = row_sums(ref, base + o + 2, cols)
            nxt2 = row_sums(ref, base + o + 3, cols)
            mid = [a + b for a, b in zip(cur, nxt)]
            extra = emit(base + o, [a + b for a, b in zip(prev, mid)], extra)
            extra = emit(base + o + 1, [a + b for a, b in zip(mid, nxt2)], extra)
            prev, cur = nxt, nxt2
        return prev, cur, extra

    zero = [jnp.zeros((SUBS, LANES), F32) for _ in range(cols)]
    first = row_sums(ref, 1, cols)
    return lax.fori_loop(0, side // chunk, body, (zero, first, carry))[2]


def one_hot(index, count):
    return (lax.broadcasted_iota(jnp.int32, (index.shape[0], count), 1) == index).astype(F32)


def exact_dot(a, b, dims):
    return lax.dot_general(a, b, (dims, ((), ())), precision=lax.Precision.HIGHEST,
                           preferred_element_type=F32)


def fold_rows(tiles):
    sub = lax.broadcasted_iota(jnp.int32, (SUBS, LANES), 0)
    shift = SUBS // 2
    while shift:
        low = sub // shift % 2 == 0
        count = len(tiles) // 2
        tiles = [jnp.where(low, x + pltpu.roll(x, SUBS - shift, 0), y + pltpu.roll(y, shift, 0))
                 for x, y in zip(tiles[:count], tiles[count:])]
        shift //= 2
    return tiles[0]


def kernel_body(dims, call, *refs):
    gs, npos, side, col_count, per_row, part = dims
    mode_ref, a_refs, b_refs = refs[0], refs[1:3], refs[3:5]
    refs = refs[5:]
    outs = 2
    if call == 1:
        before_ref = refs[0]
        refs = refs[1:]
        outs = 3
    gl_ref, gr_ref = refs[:2]
    if call == 1:
        rest_ref = refs[2]
    x_ref, v_ref, kb_ref, sg_ref, f_ref, phi_ref, sin_ref, d_ref, r_ref, w_ref, kv_ref = refs[outs:]
    feat = CHAN * npos
    own_count = per_row * part
    members = gs // own_count
    tile_rows = 2 * members * part
    rows_of_dev = 2 * tile_rows
    width = per_row * tile_rows
    total_rows = 2 * members * rows_of_dev
    rs = gs // 2
    two = 2 * gs
    cols = side // SUBS
    tiles = gs * rs // LANES
    apt = LANES // rs
    blocks = npos // LANES
    per = LANES // SUBS
    diag = mode_ref[0] == 1
    member = mode_ref[1]
    own_row, their_row = mode_ref[6], mode_ref[7]
    lane = lax.broadcasted_iota(jnp.int32, (SUBS, LANES), 1)
    sub = lax.broadcasted_iota(jnp.int32, (SUBS, LANES), 0)

    def col_of(tile):
        return tile // side, tile % side + 1

    def places(col, half, axis, first, count):
        shape = (count, 1) if axis == 0 else (1, count)
        i = lax.broadcasted_iota(jnp.int32, shape, axis) + first
        k = i // part % per_row
        idx = (half * members + jnp.bitwise_xor(member, i // own_count)) * part + i % part
        blk = k * col_count + col
        return blk, blk * tile_rows + idx, k * tile_rows + idx

    def table_place(at_row, device):
        apart = jnp.bitwise_xor(at_row // rows_of_dev, device)
        return (apart % members * 2 + apart // members) * rows_of_dev + at_row % rows_of_dev

    def pack_table(rows):
        lines = []
        for q in range(rows.shape[0] // (2 * rows_of_dev)):
            first = q * 2 * rows_of_dev
            lines.append(jnp.concatenate([rows[first + t:first + t + own_count]
                                          for t in range(0, 2 * rows_of_dev, own_count)], 1))
        return jnp.concatenate(lines, 0)

    per_line = (a_refs[0].shape[1] - feat) // width

    def packet_place(at_row, device):
        apart = jnp.bitwise_xor(at_row // rows_of_dev, device)
        within = at_row % rows_of_dev
        line = apart % members * own_count + apart // members * (own_count // 2) + within // per_line
        return within % per_line * gs + line

    def packet_table(packets):
        rows = jnp.concatenate([ref[:, feat:].astype(F32) for ref in packets], 0)
        return jnp.concatenate([rows[:, i * width:(i + 1) * width] for i in range(per_line)], 0).astype(jnp.bfloat16)

    whole_a = (mode_ref[2], mode_ref[3])
    whole_b = (mode_ref[4], mode_ref[5])
    blk_a, row_a, at_a = places(*whole_a, 0, 0, gs)
    blk_al = places(*whole_a, 1, 0, gs)[0]
    blk_r, row_r, at_r = places(*whole_b, 0, call * rs, rs)
    blk_rl = places(*whole_b, 1, call * rs, rs)[0]
    ca = packet_table(a_refs)
    cb = packet_table(b_refs)
    if call == 0:
        blk_l, row_l, at_l = places(*whole_b, 0, 0, gs)
        blk_ll = places(*whole_b, 1, 0, gs)[0]
        table_l, device_l = cb, their_row
    else:
        blk_l, row_l, at_l, blk_ll = blk_a, row_a, at_a, blk_al
        table_l, device_l = ca, own_row
    hot_at_a, hot_at_r, hot_at_l = one_hot(at_a, width), one_hot(at_r, width), one_hot(at_l, width)
    keep_ar = (blk_a <= blk_rl).astype(F32)
    keep_ra = (blk_r <= blk_al).astype(F32)
    keep_ll = (blk_l <= blk_ll).astype(F32)

    def chosen(rows, table, columns):
        picked = jnp.dot(one_hot(rows, total_rows).astype(jnp.bfloat16), table, preferred_element_type=F32)
        return lax.dot_general(picked.astype(jnp.bfloat16), columns.astype(jnp.bfloat16),
                               (((1,), (1,)), ((), ())), preferred_element_type=F32)
    w_off = (chosen(packet_place(row_a, their_row), cb, hot_at_r) * keep_ar
             + (chosen(packet_place(row_r, own_row), ca, hot_at_a) * keep_ra).T)
    w_ll = chosen(packet_place(row_l, device_l), table_l, hot_at_l) * keep_ll
    w_sym = w_ll + w_ll.T
    eye = (lax.broadcasted_iota(jnp.int32, (gs, gs), 0) == lax.broadcasted_iota(jnp.int32, (gs, gs), 1))
    half_row = lax.broadcasted_iota(jnp.int32, (rs, rs), 0)
    half_col = lax.broadcasted_iota(jnp.int32, (rs, rs), 1)
    upper, lower = half_row < half_col, half_row > half_col
    w_diag = jnp.concatenate(
        [w_sym[:rs, rs:], jnp.where(upper, w_sym[rs:, rs:], jnp.where(lower, w_sym[:rs, :rs], 0.0))], 0)
    w_all = jnp.where(diag, w_diag, w_off)
    tile_hot = one_hot(lax.broadcasted_iota(jnp.int32, (gs, 1), 0) // apt, tiles)
    lane_hot = (lax.broadcasted_iota(jnp.int32, (rs, LANES), 1) // apt
                == lax.broadcasted_iota(jnp.int32, (rs, LANES), 0)).astype(F32)
    lane_match = (lax.broadcasted_iota(jnp.int32, (gs, LANES), 1) % apt
                  == lax.broadcasted_iota(jnp.int32, (gs, LANES), 0) % apt)
    w_lanes = jnp.where(lane_match, exact_dot(w_all, lane_hot, ((1,), (0,))), 0.0)
    w_rows = exact_dot(tile_hot, w_lanes, ((0,), (0,)))
    for k in range(tiles):
        w_ref[k] = w_rows[k:k + 1]
    self_l = jnp.sum(jnp.where(eye, w_ll, 0.0), 0, keepdims=True)
    self_row = jnp.concatenate([self_l, jnp.zeros((1, LANES - gs), F32)], 1)
    self_row = jnp.where(diag, self_row, 0.0)

    zeros = jnp.zeros((SUBS, LANES), F32)
    def image_rows(sl):
        left = jnp.concatenate([ref[:, sl].astype(F32) for ref in a_refs], 0)
        if call == 0:
            left = jnp.where(diag, jnp.concatenate([ref[:, sl].astype(F32) for ref in b_refs], 0), left)
        right = jnp.where(diag, left[rs:], b_refs[call][:, sl].astype(F32))
        return jnp.concatenate([left, right, jnp.zeros((two - gs - rs, LANES), F32)], 0)

    def to_fields(x, store):
        t = jnp.concatenate([x, x], 0).T
        return [store(i, t[i * SUBS:(i + 1) * SUBS]) for i in range(per)]

    for blk in range(blocks):
        total = 0.0
        for ch in range(CHAN):
            x = image_rows(pl.ds(ch * npos + blk * LANES, LANES))
            x_ref[ch, :, pl.ds(blk * LANES, LANES)] = x
            total = total + x * x

        def store(i, t):
            j, v = col_of(blk * per + i)
            f_ref[0, j, v] = t
        to_fields(total * (1.0 / CHAN), store)
    for j in range(cols):
        for v in (0, side + 1):
            for l in range(LAYERS):
                v_ref[l, j, v] = zeros
                phi_ref[l, j, v] = zeros
            f_ref[0, j, v] = zeros
            f_ref[1, j, v] = zeros

    def block_of(ref_at, blk):
        vals = []
        for t in range(per):
            j, v = col_of(blk * per + t)
            vals.append(ref_at(j, v))
        return jnp.concatenate(vals, 0)

    def var_emit(l, scale):
        def emit(v, sums, extra):
            for j in range(cols):
                v_ref[l, j, v + 1] = sums[j] * scale + BIAS_VAR
            return extra
        return emit
    sweep(f_ref.at[0], side, cols, var_emit(0, WEIGHT_VAR / 9.0))
    sweep(v_ref.at[0], side, cols, var_emit(1, 0.5 * WEIGHT_VAR / 9.0))
    sweep(v_ref.at[1], side, cols, var_emit(2, 0.5 * WEIGHT_VAR / 9.0))
    for l in range(LAYERS):
        for blk in range(blocks):
            t = block_of(lambda j, v: v_ref[l, j, v], blk).T[:two]
            sg_ref[l, :, pl.ds(blk * LANES, LANES)] = t * lax.rsqrt(t)
    totals = [zeros] * cols
    for j in range(cols):
        for v in range(side):
            totals[j] = totals[j] + v_ref[LAYERS - 1, j, v + 1]
    kself = jnp.sum(sum(totals), 0, keepdims=True) * (0.5 * WEIGHT_VAR / npos) + BIAS_VAR

    def clear(i, _):
        sl = pl.ds(pl.multiple_of(i * LANES, LANES), LANES)
        d_ref[:, :, sl] = jnp.zeros((LAYERS + CHAN, two, LANES), F32)
        return 0
    lax.fori_loop(0, blocks, clear, 0)

    def pair_tile(k, _):
        a0 = pl.multiple_of(k * apt, SUBS)
        masked = jnp.logical_and(diag, a0 >= rs)
        lo0 = pl.multiple_of(jnp.maximum(a0 - rs, 0), SUBS)

        def put(blk, t):
            half = blk * per
            j = half // side
            v = half % side + 1
            for i in range(per):
                f_ref[0, j, v + i] = t[i * SUBS:(i + 1) * SUBS]

        def cross_plain(blk, _):
            sl = pl.ds(pl.multiple_of(blk * LANES, LANES), LANES)
            rows = []
            left = [x_ref[ch, pl.ds(a0, SUBS), sl] for ch in range(CHAN)]
            for b in range(rs):
                acc = left[0] * x_ref[0, gs + b:gs + b + 1, sl]
                for ch in range(1, CHAN):
                    acc = acc + left[ch] * x_ref[ch, gs + b:gs + b + 1, sl]
                rows.append(acc)
            put(blk, jnp.concatenate(rows, 0).T)
            return 0

        def cross_masked(blk, _):
            sl = pl.ds(pl.multiple_of(blk * LANES, LANES), LANES)
            rows = []
            left = [x_ref[ch, pl.ds(a0, SUBS), sl] for ch in range(CHAN)]
            low = [x_ref[ch, pl.ds(lo0, SUBS), sl] for ch in range(CHAN)]
            for b in range(rs):
                first = sub + lo0 < b
                acc = 0.0
                for ch in range(CHAN):
                    acc = acc + jnp.where(first, left[ch] * x_ref[ch, gs + b:gs + b + 1, sl],
                                          low[ch] * x_ref[ch, b:b + 1, sl])
                rows.append(acc)
            put(blk, jnp.concatenate(rows, 0).T)
            return 0

        @pl.when(jnp.logical_not(masked))
        def _():
            lax.fori_loop(0, blocks, cross_plain, 0, unroll=True)

        @pl.when(masked)
        def _():
            lax.fori_loop(0, blocks, cross_masked, 0, unroll=True)

        ia, ib = lane % apt, lane // apt
        second = jnp.logical_and(masked, ib <= lo0 + ia)
        il = ia + jnp.where(second, lo0, a0)
        ir = ib + jnp.where(second, 0, gs)

        @pl.when(jnp.logical_or(k == 0, masked))
        def _():
            def gather(v, _):
                for l in range(LAYERS):
                    for j in range(cols):
                        kb_ref[l, j, v] = jnp.take_along_axis(v_ref[l, j, v + 1], ir, axis=1)
                return 0
            lax.fori_loop(0, side, gather, 0, unroll=4)

        def relu_emit(l, scale, dst):
            def emit(v, sums, extra):
                for j in range(cols):
                    k12 = sums[j] * scale + BIAS_VAR
                    prod = jnp.take_along_axis(v_ref[l, j, v + 1], il, axis=1) * kb_ref[l, j, v]
                    inv = lax.rsqrt(prod)
                    cosine = k12 * inv
                    w = jnp.maximum(1.0 - jnp.abs(cosine), TINY)
                    poly = COEFFS[-1]
                    for c in COEFFS[-2::-1]:
                        poly = poly * w + c
                    angle = (w * lax.rsqrt(w)) * poly
                    phi = jnp.where(cosine >= 0.0, math.pi - angle, angle)
                    rest = jnp.maximum(prod - k12 * k12, TINY)
                    root = rest * lax.rsqrt(rest)
                    value = root + phi * k12
                    phi_ref[l, j, v + 1] = phi
                    sin_ref[l, j, v + 1] = root * inv
                    if dst is None:
                        extra = extra + value
                    else:
                        f_ref[dst, j, v + 1] = value
                return extra
            return emit

        inner = WEIGHT_VAR / (9.0 * 2.0 * math.pi)
        sweep(f_ref.at[0], side, cols, relu_emit(0, WEIGHT_VAR / (9.0 * CHAN), 1))
        sweep(f_ref.at[1], side, cols, relu_emit(1, inner, 0))
        total = sweep(f_ref.at[0], side, cols, relu_emit(2, inner, None), zeros)
        kv_ref[k] = jnp.sum(total, 0, keepdims=True) * (WEIGHT_VAR / (2.0 * math.pi * npos)) + BIAS_VAR

        wrow = jnp.broadcast_to(w_ref[k] * (WEIGHT_VAR / npos), (SUBS, LANES))
        wscaled = wrow * inner

        def back_emit(l, dst, scaled):
            def emit(v, sums, extra):
                for j in range(cols):
                    grad = sums[j] * wscaled if scaled else sums[j]
                    sin_ref[l, j, v + 1] = sin_ref[l, j, v + 1] * grad
                    f_ref[dst, j, v + 1] = phi_ref[l, j, v + 1] * grad
                return extra
            return emit
        sweep(phi_ref.at[2], side, cols, back_emit(1, 0, True))
        sweep(f_ref.at[0], side, cols, back_emit(0, 1, False))

        def last_emit(v, sums, extra):
            for j in range(cols):
                f_ref[0, j, v + 1] = sums[j]
            return extra
        sweep(f_ref.at[1], side, cols, last_emit)

        def fold(is_masked):
            def body(blk, _):
                sl = pl.ds(pl.multiple_of(blk * LANES, LANES), LANES)
                half = blk * per
                j = half // side
                v = half % side + 1

                def turned(get):
                    t = jnp.concatenate([get(j, v + i) for i in range(per)], 0).T
                    return [t[b * SUBS:(b + 1) * SUBS] for b in range(rs)]

                for l in range(LAYERS + 1):
                    if l < LAYERS - 1:
                        h = turned(lambda j, v: sin_ref[l, j, v])
                    elif l == LAYERS - 1:
                        h = turned(lambda j, v: sin_ref[l, j, v] * wrow)
                    else:
                        h = turned(lambda j, v: f_ref[0, j, v])
                    terms = [(l, sg_ref, l)] if l < LAYERS else [(LAYERS + ch, x_ref, ch) for ch in range(CHAN)]
                    if is_masked:
                        first = [jnp.where(sub + lo0 < b, h[b], 0.0) for b in range(rs)]
                        other = [jnp.where(sub + lo0 > b, h[b], 0.0) for b in range(rs)]
                    for slot, src, at in terms:
                        left = src[at, pl.ds(a0, SUBS), sl]
                        total = 0.0
                        if is_masked:
                            low = src[at, pl.ds(lo0, SUBS), sl]
                            low_total = 0.0
                            for b in range(rs):
                                total = total + first[b] * src[at, gs + b:gs + b + 1, sl]
                                low_total = low_total + other[b] * src[at, b:b + 1, sl]
                                r_ref[k, slot, b, :, sl] = first[b] * left + other[b] * low
                            d_ref[slot, pl.ds(lo0, SUBS), sl] = d_ref[slot, pl.ds(lo0, SUBS), sl] + low_total
                        else:
                            for b in range(rs):
                                total = total + h[b] * src[at, gs + b:gs + b + 1, sl]
                                r_ref[k, slot, b, :, sl] = h[b] * left
                        d_ref[slot, pl.ds(a0, SUBS), sl] = d_ref[slot, pl.ds(a0, SUBS), sl] + total
                return 0
            lax.fori_loop(0, blocks, body, 0, unroll=True)

        @pl.when(jnp.logical_not(masked))
        def _():
            fold(False)

        @pl.when(masked)
        def _():
            fold(True)
        return 0

    lax.fori_loop(0, tiles, pair_tile, 0)

    def gather_right(low):
        def body(blk, _):
            sl = pl.ds(pl.multiple_of(blk * LANES, LANES), LANES)
            for slot in range(LAYERS + CHAN):
                for b0 in range(0, rs, SUBS):
                    sums = []
                    for b in range(b0, b0 + SUBS):
                        t = 0.0
                        for k in range(tiles):
                            if low is None:
                                t = t + r_ref[k, slot, b, :, sl]
                            elif k * apt < rs:
                                t = t if low else t + r_ref[k, slot, b, :, sl]
                            else:
                                i = sub + (k * apt - rs)
                                t = t + jnp.where(i > b if low else i < b, r_ref[k, slot, b, :, sl], 0.0)
                        sums.append(t)
                    at = pl.ds(b0 if low else gs + b0, SUBS)
                    d_ref[slot, at, sl] = d_ref[slot, at, sl] + fold_rows(sums)
            return 0
        lax.fori_loop(0, blocks, body, 0, unroll=2)

    @pl.when(jnp.logical_not(diag))
    def _():
        gather_right(None)

    @pl.when(diag)
    def _():
        gather_right(0)
        gather_right(1)

    step = WEIGHT_VAR / (9.0 * 2.0 * math.pi)
    selfw = self_row * (0.5 * WEIGHT_VAR / npos)
    for l in range(LAYERS):
        dest = phi_ref if l == LAYERS - 1 else sin_ref
        scale = (step if l == 0 else 1.0) / (4.0 * math.pi)
        for blk in range(blocks):
            def store(i, t):
                j, v = col_of(blk * per + i)
                t = t * (lax.rsqrt(v_ref[l, j, v]) * scale)
                dest[l, j, v] = t + selfw if l == LAYERS - 1 else t
            to_fields(d_ref[l, :, pl.ds(blk * LANES, LANES)], store)

    def chain_emit(l):
        def emit(v, sums, extra):
            for j in range(cols):
                phi_ref[l, j, v + 1] = sin_ref[l, j, v + 1] + sums[j] * (0.5 * WEIGHT_VAR / 9.0)
            return extra
        return emit
    sweep(phi_ref.at[2], side, cols, chain_emit(1))
    sweep(phi_ref.at[1], side, cols, chain_emit(0))

    def final_emit(v, sums, extra):
        for j in range(cols):
            f_ref[0, j, v + 1] = sums[j] * (WEIGHT_VAR / 9.0 * 2.0 / CHAN)
        return extra
    sweep(phi_ref.at[0], side, cols, final_emit)
    for blk in range(blocks):
        e = block_of(lambda j, v: f_ref[0, j, v], blk).T[:two]
        at = pl.ds(blk * LANES, LANES)
        for ch in range(CHAN):
            sl = pl.ds(ch * npos + blk * LANES, LANES)
            grad = d_ref[LAYERS + ch, :, at] * (step * step / CHAN) + x_ref[ch, :, at] * e
            right = grad[gs:gs + rs]
            left = jnp.concatenate([grad[:rs], grad[rs:gs] + jnp.where(diag, right, 0.0)], 0)
            if call == 0:
                gl_ref[:, sl] = left
                gr_ref[:, sl] = jnp.where(diag, left[:rs], right)
            else:
                before = before_ref[:, sl]
                gl_ref[:, sl] = left + jnp.where(diag, 0.0, before)
                gr_ref[:, sl] = jnp.where(diag, before[rs:], right)

    kv = jnp.concatenate([kv_ref[k] for k in range(tiles)], 0)
    values = exact_dot(jnp.where(lane_match, exact_dot(tile_hot, kv, ((1,), (0,))), 0.0), lane_hot, ((1,), (1,)))
    across, within = values[:rs], values[rs:]
    low_part, high_part = jnp.where(lower, within, 0.0), jnp.where(upper, within, 0.0)
    val_ll = jnp.concatenate([jnp.concatenate([low_part + low_part.T, across], 1),
                              jnp.concatenate([across.T, high_part + high_part.T], 1)], 0)
    val_ll = jnp.where(eye, kself[:, :gs], val_ll) * keep_ll

    def spread(rows, vals, columns):
        return exact_dot(one_hot(rows, total_rows), exact_dot(vals, columns, ((1,), (0,))), ((0,), (0,)))
    far_row = jnp.bitwise_xor(their_row, members // 2)
    rows_l, rows_a = table_place(row_l, far_row if call == 0 else own_row), table_place(row_a, far_row)
    diagonal = spread(rows_l, val_ll, hot_at_l)
    ours = spread(table_place(row_r, own_row), values.T * keep_ra, hot_at_a)
    theirs = spread(rows_a, values * keep_ar, hot_at_r)
    ours = jnp.where(diag, 0.0 if call == 0 else diagonal, ours)
    theirs = jnp.where(diag, diagonal if call == 0 else 0.0, theirs)
    ours = pack_table(ours)
    theirs = pack_table(theirs)
    if call == 0:
        gl_ref[:, feat:] = ours
        gr_ref[:, feat:] = jnp.concatenate([theirs[rs:], theirs[:rs]], 1)
    else:
        gl_ref[:, feat:] = ours + before_ref[:, feat:]
        gr_ref[:, feat:] = theirs[:rs]
        rest_ref[...] = theirs[rs:]


def pair_kernel(call, mode, packets, dims, before=()):
    gs, npos, side, col_count, per_row, part = dims
    cols = side // SUBS
    tiles = gs * gs // 2 // LANES
    terms = LAYERS + CHAN
    field = (cols, side + 2, SUBS, LANES)
    feat = CHAN * npos
    tile_rows = 2 * gs // per_row
    lines = 4 * tile_rows * per_row * tile_rows // (per_row * part)
    rs = gs // 2
    shapes = [(gs, feat + lines)] + ([(rs, feat + 2 * lines)] if call == 0 else [(rs, feat + lines), (rs, lines)])
    vm = pl.BlockSpec(memory_space=pltpu.VMEM)
    operands = (mode, *packets, *before)
    return pl.pallas_call(
        functools.partial(kernel_body, dims, call),
        out_shape=[jax.ShapeDtypeStruct(shape, F32) for shape in shapes],
        in_specs=[pl.BlockSpec(memory_space=pltpu.SMEM)] + [vm] * (len(operands) - 1),
        out_specs=[vm] * len(shapes),
        scratch_shapes=[
            pltpu.VMEM((CHAN, 2 * gs, npos), F32),
            pltpu.VMEM((LAYERS,) + field, F32),
            pltpu.VMEM((LAYERS, cols, side, SUBS, LANES), F32),
            pltpu.VMEM((LAYERS, 2 * gs, npos), F32),
            pltpu.VMEM((2,) + field, F32),
            pltpu.VMEM((LAYERS,) + field, F32),
            pltpu.VMEM((LAYERS,) + field, F32),
            pltpu.VMEM((terms, 2 * gs, npos), F32),
            pltpu.VMEM((tiles, terms, rs, SUBS, npos), F32),
            pltpu.VMEM((tiles, 1, LANES), F32),
            pltpu.VMEM((tiles, 1, LANES), F32),
        ],
        compiler_params=pltpu.CompilerParams(vmem_limit_bytes=40 * 1024 * 1024),
        cost_estimate=pl.CostEstimate(flops=2 * 10**10, bytes_accessed=5 * 10**7, transcendentals=10**6),
        name="pair_fields",
    )(*operands)


def exchange(x, rows, cols, target):
    perm = []
    for r in range(rows):
        for c in range(cols):
            tr, tc = target(r, c)
            perm.append((r * cols + c, tr * cols + tc))
    return lax.ppermute(x, ("row", "col"), perm)


def body(images, cotangent):
    rows = lax.axis_size("row")
    cols = lax.axis_size("col")
    row = lax.axis_index("row")
    col = lax.axis_index("col")
    per_row, _, part, feat = images.shape
    members = rows // 2
    groups = 2 * cols
    assert members == cols and members & (members - 1) == 0
    tile_rows = part * rows
    npos = feat // CHAN
    side = math.isqrt(npos)
    count = per_row * part
    gs = members * count
    own = images.reshape(count * CHAN, SUBS, npos // SUBS).transpose(0, 2, 1).reshape(count, feat)

    def partner_of(r, c, flip=0, turn=0):
        half, m = r // members, r % members
        other = (half * cols + c + 1 + m) % groups
        return (other // cols ^ turn) * members + (m ^ flip), other % cols

    holders = {}
    for r in range(rows):
        for c in range(cols):
            holders[partner_of(r, c)] = (r, c)

    def holder_of(r, c, flip=0, turn=0):
        return holders[r ^ flip ^ turn * members, c]

    def swap(x, bit):
        return exchange(x, rows, cols, lambda r, c: (r ^ bit, c))

    cot_own = cotangent.reshape(count // 2, -1)
    packet = jnp.concatenate([own, jnp.concatenate([cot_own, swap(cot_own, members)], 0)], 1)
    bits = []
    while 1 << len(bits) < members:
        bits.append(1 << len(bits))
    near, last = packet, bits[-1]
    for bit in bits[:-1]:
        near = jnp.concatenate([near, swap(near, bit)], 0)
    packets = [near, swap(near, last)]
    packets += [exchange(near, rows, cols, functools.partial(holder_of, flip=f)) for f in (0, last)]
    p_row, p_col = partner_of(row, col)
    member = row % members
    half = row // members
    diag = jnp.logical_and(member == members - 1, half == 1)
    mode = jnp.stack([diag.astype(jnp.int32), member, col, half, p_col, p_row // members, row, p_row])
    mode = mode.astype(jnp.int32)

    dims = (gs, npos, side, cols, per_row, part)
    half_count = gs // 2
    gl, gr = pair_kernel(0, mode, packets, dims)
    first = exchange(gr, rows, cols, functools.partial(partner_of, flip=last))
    gl, gr, rest = pair_kernel(1, mode, packets, dims, before=(gl,))
    lines = rest.shape[1]
    gr = exchange(gr, rows, cols, functools.partial(partner_of, flip=last))
    rest = exchange(rest, rows, cols, partner_of)
    met = swap(gl[half_count:] + first[:, :feat + lines], last)
    out = gl[:half_count] + met + gr + jnp.pad(first[:, feat + lines:] + rest, ((0, 0), (feat, 0)))
    for bit in bits[-2::-1]:
        n = out.shape[0] // 2
        out = out[:n] + swap(out[n:], bit)
    table = out[:, feat:]
    n = lines // 2
    table = table[:, :n] + swap(table[:, n:], members)
    width = per_row * tile_rows
    table = table.reshape(count, n // width, width).transpose(1, 0, 2)
    grads = out[:, :feat].reshape(count * CHAN, npos // SUBS, SUBS).transpose(0, 2, 1)
    return (table.reshape(2, tile_rows, per_row, 1, tile_rows),
            grads.reshape(per_row, 1, part, feat))


def solution(mesh):
    return jax.shard_map(
        body,
        mesh=mesh,
        in_specs=(P(None, "col", "row", None), P("row", None, None, "col", None)),
        out_specs=(P("row", None, None, "col", None), P(None, "col", "row", None)),
        check_vma=False,
    )
```

```python
import functools, math
import jax, jax.numpy as jnp, numpy as np
from jax import lax
from jax.experimental import pallas as pl
from jax.experimental.pallas import tpu as pltpu
from jax.sharding import PartitionSpec as P

CHAN = 3
LAYERS = 3
WEIGHT_VAR = 2.0
BIAS_VAR = 0.1
LANES = 128
SUBS = 8
TINY = 1e-30
F32 = jnp.float32


def arccos_coefficients(degree):
    nodes = 0.5 + 0.5 * np.cos(np.pi * (np.arange(400) + 0.5) / 400)
    target = np.arccos(1.0 - nodes) / np.sqrt(nodes)
    fit = np.polynomial.chebyshev.Chebyshev.fit(nodes, target, degree, domain=[0.0, 1.0])
    return [float(c) for c in fit.convert(kind=np.polynomial.Polynomial).coef]


COEFFS = arccos_coefficients(5)


def row_sums(ref, v, cols):
    f = [ref[j, v] for j in range(cols)]
    sub = lax.broadcasted_iota(jnp.int32, (SUBS, LANES), 0)
    above = jnp.where(sub > 0, pltpu.roll(f[-1], 1, 0), 0.0)
    below = jnp.where(sub < SUBS - 1, pltpu.roll(f[0], SUBS - 1, 0), 0.0)
    g = [above] + f + [below]
    out = []
    for j in range(0, cols, 2):
        mid = g[j + 1] + g[j + 2]
        out.append(g[j] + mid)
        out.append(mid + g[j + 3])
    return out


def sweep(ref, side, cols, emit, carry=(), chunk=32):
    def body(i, state):
        prev, cur, extra = state
        base = i * chunk
        for o in range(0, chunk, 2):
            nxt = row_sums(ref, base + o + 2, cols)
            nxt2 = row_sums(ref, base + o + 3, cols)
            mid = [a + b for a, b in zip(cur, nxt)]
            extra = emit(base + o, [a + b for a, b in zip(prev, mid)], extra)
            extra = emit(base + o + 1, [a + b for a, b in zip(mid, nxt2)], extra)
            prev, cur = nxt, nxt2
        return prev, cur, extra

    zero = [jnp.zeros((SUBS, LANES), F32) for _ in range(cols)]
    first = row_sums(ref, 1, cols)
    return lax.fori_loop(0, side // chunk, body, (zero, first, carry))[2]


def one_hot(index, count):
    return (lax.broadcasted_iota(jnp.int32, (index.shape[0], count), 1) == index).astype(F32)


def pick(hot, values, dims):
    high = values.astype(jnp.bfloat16)
    rest = values - high.astype(F32)
    mid = rest.astype(jnp.bfloat16)
    low = (rest - mid.astype(F32)).astype(jnp.bfloat16)
    hot = hot.astype(jnp.bfloat16)
    (left,), (right,) = dims
    return lax.dot_general(jnp.concatenate([hot] * 3, left), jnp.concatenate([high, mid, low], right),
                           (dims, ((), ())), preferred_element_type=F32)


def fold_rows(tiles):
    sub = lax.broadcasted_iota(jnp.int32, (SUBS, LANES), 0)
    shift = SUBS // 2
    while shift:
        low = sub // shift % 2 == 0
        count = len(tiles) // 2
        tiles = [jnp.where(low, x + pltpu.roll(x, SUBS - shift, 0), y + pltpu.roll(y, shift, 0))
                 for x, y in zip(tiles[:count], tiles[count:])]
        shift //= 2
    return tiles[0]


def kernel_body(dims, call, *refs):
    gs, npos, side, col_count, per_row, part = dims
    mode_ref, a_refs, b_refs = refs[0], refs[1:3], refs[3:5]
    refs = refs[5:]
    if call == 1:
        before_l_ref, before_r_ref = refs[:2]
        refs = refs[2:]
    gl_ref, gr_ref, rest_ref = refs[:3]
    x_ref, v_ref, kb_ref, sg_ref, f_ref, phi_ref, sin_ref, d_ref, r_ref, w_ref, kv_ref = refs[3:]
    feat = CHAN * npos
    own_count = per_row * part
    members = gs // own_count
    tile_rows = 2 * members * part
    rows_of_dev = 2 * tile_rows
    width = per_row * tile_rows
    total_rows = 2 * members * rows_of_dev
    rs = gs // 2
    two = 2 * gs
    cols = side // SUBS
    tiles = gs * rs // LANES
    apt = LANES // rs
    blocks = npos // LANES
    per = LANES // SUBS
    flag = mode_ref[0] == 1
    diag = flag if call == 1 else None
    swapped = jnp.logical_and(flag, mode_ref[3] == 1)
    member = mode_ref[1]
    own_row, their_row = mode_ref[6], mode_ref[7]
    lane = lax.broadcasted_iota(jnp.int32, (SUBS, LANES), 1)
    sub = lax.broadcasted_iota(jnp.int32, (SUBS, LANES), 0)

    def col_of(tile):
        return tile // side, tile % side + 1

    def places(col, half, axis, first, count):
        shape = (count, 1) if axis == 0 else (1, count)
        i = lax.broadcasted_iota(jnp.int32, shape, axis) + first
        k = i // part % per_row
        idx = (half * members + jnp.bitwise_xor(member, i // own_count)) * part + i % part
        blk = k * col_count + col
        return blk, blk * tile_rows + idx, k * tile_rows + idx

    def table_place(at_row, device):
        apart = jnp.bitwise_xor(at_row // rows_of_dev, device)
        return (apart % members * 2 + apart // members) * rows_of_dev + at_row % rows_of_dev

    def pack_table(rows):
        lines = []
        for q in range(rows.shape[0] // (2 * rows_of_dev)):
            first = q * 2 * rows_of_dev
            lines.append(jnp.concatenate([rows[first + t:first + t + own_count]
                                          for t in range(0, 2 * rows_of_dev, own_count)], 1))
        return jnp.concatenate(lines, 0)

    per_line = (a_refs[0].shape[1] - feat) // width

    def packet_place(at_row, device):
        apart = jnp.bitwise_xor(at_row // rows_of_dev, device)
        within = at_row % rows_of_dev
        line = apart % members * own_count + apart // members * (own_count // 2) + within // per_line
        return within % per_line * gs + line

    def packet_table(packets):
        rows = jnp.concatenate([ref[:, feat:].astype(F32) for ref in packets], 0)
        return jnp.concatenate([rows[:, i * width:(i + 1) * width] for i in range(per_line)], 0).astype(jnp.bfloat16)

    ours_at = (mode_ref[2], mode_ref[3], own_row)
    theirs_at = (mode_ref[4], mode_ref[5], their_row)
    ca = packet_table(a_refs)
    cb = packet_table(b_refs)
    if call == 0:
        col_l, half_l, device_l = [jnp.where(swapped, t, o) for o, t in zip(ours_at, theirs_at)]
        col_r, half_r, device_r = [jnp.where(swapped, o, t) for o, t in zip(ours_at, theirs_at)]
        first_r = jnp.where(swapped, 0, rs)
        table_l, table_r = jnp.where(swapped, cb, ca), jnp.where(swapped, ca, cb)
    else:
        (col_l, half_l, device_l), (col_r, half_r, device_r) = ours_at, theirs_at
        first_r = 0
        table_l, table_r = ca, cb
    blk_l, row_l, at_l = places(col_l, half_l, 0, 0, gs)
    blk_ll = places(col_l, half_l, 1, 0, gs)[0]
    blk_r, row_r, at_r = places(col_r, half_r, 0, first_r, rs)
    blk_rl = places(col_r, half_r, 1, first_r, rs)[0]
    hot_at_l, hot_at_r = one_hot(at_l, width), one_hot(at_r, width)
    keep_lr = (blk_l <= blk_rl).astype(F32)
    keep_rl = (blk_r <= blk_ll).astype(F32)

    def chosen(rows, table, columns):
        picked = jnp.dot(one_hot(rows, total_rows).astype(jnp.bfloat16), table.astype(jnp.bfloat16),
                         preferred_element_type=F32)
        return lax.dot_general(picked.astype(jnp.bfloat16), columns.astype(jnp.bfloat16),
                               (((1,), (1,)), ((), ())), preferred_element_type=F32)
    w_all = (chosen(packet_place(row_l, device_r), table_r, hot_at_r) * keep_lr
             + (chosen(packet_place(row_r, device_l), table_l, hot_at_l) * keep_rl).T)
    if call == 1:
        keep_ll = (blk_l <= blk_ll).astype(F32)
        w_ll = chosen(packet_place(row_l, device_l), table_l, hot_at_l) * keep_ll
        w_sym = w_ll + w_ll.T
        eye = (lax.broadcasted_iota(jnp.int32, (gs, gs), 0) == lax.broadcasted_iota(jnp.int32, (gs, gs), 1))
        half_row = lax.broadcasted_iota(jnp.int32, (rs, rs), 0)
        half_col = lax.broadcasted_iota(jnp.int32, (rs, rs), 1)
        upper, lower = half_row < half_col, half_row > half_col
        w_diag = jnp.concatenate(
            [w_sym[:rs, rs:], jnp.where(upper, w_sym[rs:, rs:], jnp.where(lower, w_sym[:rs, :rs], 0.0))], 0)
        w_all = jnp.where(diag, w_diag, w_all)
        self_l = jnp.sum(jnp.where(eye, w_ll, 0.0), 0, keepdims=True)
        self_row = jnp.concatenate([self_l, jnp.zeros((1, LANES - gs), F32)], 1)
        self_row = jnp.where(diag, self_row, 0.0)
    tile_hot = one_hot(lax.broadcasted_iota(jnp.int32, (gs, 1), 0) // apt, tiles)
    lane_hot = (lax.broadcasted_iota(jnp.int32, (rs, LANES), 1) // apt
                == lax.broadcasted_iota(jnp.int32, (rs, LANES), 0)).astype(F32)
    lane_match = (lax.broadcasted_iota(jnp.int32, (gs, LANES), 1) % apt
                  == lax.broadcasted_iota(jnp.int32, (gs, LANES), 0) % apt)
    w_lanes = jnp.where(lane_match, pick(lane_hot.T, w_all.T, ((1,), (0,))).T, 0.0)
    w_rows = pick(tile_hot.T, w_lanes, ((1,), (0,)))
    for k in range(tiles):
        w_ref[k] = w_rows[k:k + 1]
    zeros = jnp.zeros((SUBS, LANES), F32)
    def image_rows(sl):
        a = [ref[:, sl].astype(F32) for ref in a_refs]
        if call == 0:
            b = [ref[:, sl].astype(F32) for ref in b_refs]
            left = jnp.where(swapped, jnp.concatenate(b, 0), jnp.concatenate(a, 0))
            right = jnp.where(swapped, a[0], b[1])
        else:
            left = jnp.concatenate(a, 0)
            right = jnp.where(diag, a[1], b_refs[0][:, sl].astype(F32))
        return jnp.concatenate([left, right, jnp.zeros((two - gs - rs, LANES), F32)], 0)

    def to_fields(x, store):
        t = jnp.concatenate([x, x], 0).T
        return [store(i, t[i * SUBS:(i + 1) * SUBS]) for i in range(per)]

    for blk in range(blocks):
        total = 0.0
        for ch in range(CHAN):
            x = image_rows(pl.ds(ch * npos + blk * LANES, LANES))
            x_ref[ch, :, pl.ds(blk * LANES, LANES)] = x
            total = total + x * x

        def store(i, t):
            j, v = col_of(blk * per + i)
            f_ref[0, j, v] = t
        to_fields(total * (1.0 / CHAN), store)
    for j in range(cols):
        for v in (0, side + 1):
            for l in range(LAYERS):
                v_ref[l, j, v] = zeros
                phi_ref[l, j, v] = zeros
            f_ref[0, j, v] = zeros
            f_ref[1, j, v] = zeros

    def block_of(ref_at, blk):
        vals = []
        for t in range(per):
            j, v = col_of(blk * per + t)
            vals.append(ref_at(j, v))
        return jnp.concatenate(vals, 0)

    inner = WEIGHT_VAR / (9.0 * 2.0 * math.pi)
    scales = [WEIGHT_VAR / (9.0 * CHAN)]
    while len(scales) < LAYERS:
        scales.append(scales[-1] * inner)

    def var_emit(l, scale):
        def emit(v, sums, extra):
            for j in range(cols):
                v_ref[l, j, v + 1] = sums[j] * (scale / scales[l]) + BIAS_VAR / scales[l]
            return extra
        return emit
    sweep(f_ref.at[0], side, cols, var_emit(0, WEIGHT_VAR / 9.0))
    for l in range(1, LAYERS):
        sweep(v_ref.at[l - 1], side, cols, var_emit(l, 0.5 * WEIGHT_VAR / 9.0 * scales[l - 1]))
    for l in range(LAYERS):
        for blk in range(blocks):
            t = block_of(lambda j, v: v_ref[l, j, v], blk).T[:two]
            sg_ref[l, :, pl.ds(blk * LANES, LANES)] = t * lax.rsqrt(t)
    totals = [zeros] * cols
    for j in range(cols):
        for v in range(side):
            totals[j] = totals[j] + v_ref[LAYERS - 1, j, v + 1]
    kself = jnp.sum(sum(totals), 0, keepdims=True) * (0.5 * WEIGHT_VAR / npos * scales[-1]) + BIAS_VAR

    def clear(i, _):
        sl = pl.ds(pl.multiple_of(i * LANES, LANES), LANES)
        d_ref[:, :, sl] = jnp.zeros((LAYERS + CHAN, two, LANES), F32)
        return 0
    lax.fori_loop(0, blocks, clear, 0)

    def pair_tile(k, _):
        a0 = pl.multiple_of(k * apt, SUBS)
        masked = jnp.logical_and(diag, a0 >= rs) if call == 1 else False
        lo0 = pl.multiple_of(jnp.maximum(a0 - rs, 0), SUBS)

        def put(blk, t):
            half = blk * per
            j = half // side
            v = half % side + 1
            for i in range(per):
                f_ref[0, j, v + i] = t[i * SUBS:(i + 1) * SUBS]

        def cross_plain(blk, _):
            sl = pl.ds(pl.multiple_of(blk * LANES, LANES), LANES)
            rows = []
            left = [x_ref[ch, pl.ds(a0, SUBS), sl] for ch in range(CHAN)]
            for b in range(rs):
                acc = left[0] * x_ref[0, gs + b:gs + b + 1, sl]
                for ch in range(1, CHAN):
                    acc = acc + left[ch] * x_ref[ch, gs + b:gs + b + 1, sl]
                rows.append(acc)
            put(blk, jnp.concatenate(rows, 0).T)
            return 0

        def cross_masked(blk, _):
            sl = pl.ds(pl.multiple_of(blk * LANES, LANES), LANES)
            rows = []
            left = [x_ref[ch, pl.ds(a0, SUBS), sl] for ch in range(CHAN)]
            low = [x_ref[ch, pl.ds(lo0, SUBS), sl] for ch in range(CHAN)]
            for b in range(rs):
                first = sub + lo0 < b
                acc = 0.0
                for ch in range(CHAN):
                    acc = acc + jnp.where(first, left[ch] * x_ref[ch, gs + b:gs + b + 1, sl],
                                          low[ch] * x_ref[ch, b:b + 1, sl])
                rows.append(acc)
            put(blk, jnp.concatenate(rows, 0).T)
            return 0

        def either(plain, with_mask):
            if call == 0:
                plain()
                return

            @pl.when(jnp.logical_not(masked))
            def _():
                plain()

            @pl.when(masked)
            def _():
                with_mask()

        either(lambda: lax.fori_loop(0, blocks, cross_plain, 0, unroll=True),
               lambda: lax.fori_loop(0, blocks, cross_masked, 0, unroll=True))

        ia, ib = lane % apt, lane // apt
        il, ir = ia + a0, ib + gs
        if call == 1:
            second = jnp.logical_and(masked, ib <= lo0 + ia)
            il = jnp.where(second, ia + lo0, il)
            ir = jnp.where(second, ib, ir)

        @pl.when(jnp.logical_or(k == 0, masked) if call == 1 else k == 0)
        def _():
            def gather(v, _):
                for l in range(LAYERS):
                    for j in range(cols):
                        kb_ref[l, j, v] = jnp.take_along_axis(v_ref[l, j, v + 1], ir, axis=1)
                return 0
            lax.fori_loop(0, side, gather, 0, unroll=True)

        def relu_emit(l, dst):
            def emit(v, sums, extra):
                for j in range(cols):
                    k12 = sums[j] + BIAS_VAR / scales[l]
                    prod = jnp.take_along_axis(v_ref[l, j, v + 1], il, axis=1) * kb_ref[l, j, v]
                    inv = lax.rsqrt(prod)
                    cosine = k12 * inv
                    w = jnp.maximum(1.0 - jnp.abs(cosine), TINY)
                    poly = COEFFS[-1]
                    for c in COEFFS[-2::-1]:
                        poly = poly * w + c
                    angle = (w * lax.rsqrt(w)) * poly
                    phi = jnp.where(cosine >= 0.0, math.pi - angle, angle)
                    rest = jnp.maximum(prod - k12 * k12, TINY)
                    root = rest * lax.rsqrt(rest)
                    value = root + phi * k12
                    phi_ref[l, j, v + 1] = phi
                    sin_ref[l, j, v + 1] = root * inv
                    if dst is None:
                        extra = extra + value
                    else:
                        f_ref[dst, j, v + 1] = value
                return extra
            return emit

        sweep(f_ref.at[0], side, cols, relu_emit(0, 1))
        sweep(f_ref.at[1], side, cols, relu_emit(1, 0))
        total = sweep(f_ref.at[0], side, cols, relu_emit(2, None), zeros)
        kv_ref[k] = jnp.sum(total, 0, keepdims=True) * (WEIGHT_VAR / (2.0 * math.pi * npos) * scales[-1]) + BIAS_VAR

        wrow = jnp.broadcast_to(w_ref[k] * (WEIGHT_VAR / npos), (SUBS, LANES))
        wscaled = wrow * inner

        def back_emit(l, dst, scaled):
            def emit(v, sums, extra):
                for j in range(cols):
                    grad = sums[j] * wscaled if scaled else sums[j]
                    sin_ref[l, j, v + 1] = sin_ref[l, j, v + 1] * grad
                    f_ref[dst, j, v + 1] = phi_ref[l, j, v + 1] * grad
                return extra
            return emit
        sweep(phi_ref.at[2], side, cols, back_emit(1, 0, True))
        sweep(f_ref.at[0], side, cols, back_emit(0, 1, False))

        def last_emit(v, sums, extra):
            for j in range(cols):
                f_ref[0, j, v + 1] = sums[j]
            return extra
        sweep(f_ref.at[1], side, cols, last_emit)

        def fold(is_masked):
            def body(blk, _):
                sl = pl.ds(pl.multiple_of(blk * LANES, LANES), LANES)
                half = blk * per
                j = half // side
                v = half % side + 1

                def turned(get):
                    t = jnp.concatenate([get(j, v + i) for i in range(per)], 0).T
                    return [t[b * SUBS:(b + 1) * SUBS] for b in range(rs)]

                for l in range(LAYERS + 1):
                    if l < LAYERS - 1:
                        h = turned(lambda j, v: sin_ref[l, j, v])
                    elif l == LAYERS - 1:
                        h = turned(lambda j, v: sin_ref[l, j, v] * wrow)
                    else:
                        h = turned(lambda j, v: f_ref[0, j, v])
                    terms = [(l, sg_ref, l)] if l < LAYERS else [(LAYERS + ch, x_ref, ch) for ch in range(CHAN)]
                    if is_masked:
                        first = [jnp.where(sub + lo0 < b, h[b], 0.0) for b in range(rs)]
                        other = [jnp.where(sub + lo0 > b, h[b], 0.0) for b in range(rs)]
                    for slot, src, at in terms:
                        left = src[at, pl.ds(a0, SUBS), sl]
                        total = 0.0
                        if is_masked:
                            low = src[at, pl.ds(lo0, SUBS), sl]
                            low_total = 0.0
                            for b in range(rs):
                                total = total + first[b] * src[at, gs + b:gs + b + 1, sl]
                                low_total = low_total + other[b] * src[at, b:b + 1, sl]
                                r_ref[k, slot, b, :, sl] = first[b] * left + other[b] * low
                            d_ref[slot, pl.ds(lo0, SUBS), sl] = d_ref[slot, pl.ds(lo0, SUBS), sl] + low_total
                        else:
                            for b in range(rs):
                                total = total + h[b] * src[at, gs + b:gs + b + 1, sl]
                                r_ref[k, slot, b, :, sl] = h[b] * left
                        d_ref[slot, pl.ds(a0, SUBS), sl] = d_ref[slot, pl.ds(a0, SUBS), sl] + total
                return 0
            lax.fori_loop(0, blocks, body, 0, unroll=True)

        either(lambda: fold(False), lambda: fold(True))
        return 0

    lax.fori_loop(0, tiles, pair_tile, 0)

    def gather_right(low):
        def body(blk, _):
            sl = pl.ds(pl.multiple_of(blk * LANES, LANES), LANES)
            for slot in range(LAYERS + CHAN):
                for b0 in range(0, rs, SUBS):
                    sums = []
                    for b in range(b0, b0 + SUBS):
                        t = 0.0
                        for k in range(tiles):
                            if low is None:
                                t = t + r_ref[k, slot, b, :, sl]
                            elif k * apt < rs:
                                t = t if low else t + r_ref[k, slot, b, :, sl]
                            else:
                                i = sub + (k * apt - rs)
                                t = t + jnp.where(i > b if low else i < b, r_ref[k, slot, b, :, sl], 0.0)
                        sums.append(t)
                    at = pl.ds(b0 if low else gs + b0, SUBS)
                    d_ref[slot, at, sl] = d_ref[slot, at, sl] + fold_rows(sums)
            return 0
        lax.fori_loop(0, blocks, body, 0, unroll=True)

    if call == 0:
        gather_right(None)
    else:
        @pl.when(jnp.logical_not(diag))
        def _():
            gather_right(None)

        @pl.when(diag)
        def _():
            gather_right(0)
            gather_right(1)

    selfw = self_row * (0.5 * WEIGHT_VAR / npos) if call == 1 else 0.0
    for l in range(LAYERS):
        dest = phi_ref if l == LAYERS - 1 else sin_ref
        scale = (inner if l == 0 else 1.0) / (4.0 * math.pi)
        for blk in range(blocks):
            def store(i, t):
                j, v = col_of(blk * per + i)
                t = t * (lax.rsqrt(v_ref[l, j, v]) * scale)
                dest[l, j, v] = t + selfw if l == LAYERS - 1 else t
            to_fields(d_ref[l, :, pl.ds(blk * LANES, LANES)], store)

    def chain_emit(l):
        def emit(v, sums, extra):
            for j in range(cols):
                phi_ref[l, j, v + 1] = sin_ref[l, j, v + 1] + sums[j] * (0.5 * WEIGHT_VAR / 9.0)
            return extra
        return emit
    sweep(phi_ref.at[2], side, cols, chain_emit(1))
    sweep(phi_ref.at[1], side, cols, chain_emit(0))

    def final_emit(v, sums, extra):
        for j in range(cols):
            f_ref[0, j, v + 1] = sums[j] * (WEIGHT_VAR / 9.0 * 2.0 / CHAN)
        return extra
    sweep(phi_ref.at[0], side, cols, final_emit)
    for blk in range(blocks):
        e = block_of(lambda j, v: f_ref[0, j, v], blk).T[:two]
        at = pl.ds(blk * LANES, LANES)
        for ch in range(CHAN):
            sl = pl.ds(ch * npos + blk * LANES, LANES)
            grad = d_ref[LAYERS + ch, :, at] * (inner * inner / CHAN) + x_ref[ch, :, at] * e
            left, right = grad[:gs], grad[gs:gs + rs]
            if call == 0:
                near = jnp.where(swapped, right, left[:rs])
                gl_ref[:, sl] = jnp.concatenate([near, jnp.where(swapped, 0.0, left[rs:])], 0)
                gr_ref[:, sl] = jnp.where(swapped, left[rs:], right)
                rest_ref[:, sl] = jnp.where(swapped, left[:rs], 0.0)
            else:
                far = left[rs:] + jnp.where(diag, right, 0.0)
                gl_ref[:, sl] = jnp.concatenate([left[:rs], far], 0) + before_l_ref[:, sl]
                gr_ref[:, sl] = jnp.where(diag, before_r_ref[:, sl], right)

    kv = jnp.concatenate([kv_ref[k] for k in range(tiles)], 0)
    values = pick(lane_hot, jnp.where(lane_match, pick(tile_hot, kv, ((1,), (0,))), 0.0).T, ((1,), (0,))).T

    def spread(rows, vals, columns):
        placed = pick(columns.T, vals.T, ((1,), (0,))).T
        return pick(one_hot(rows, total_rows).T, placed, ((1,), (0,)))
    if call == 0:
        in_l = spread(table_place(row_r, device_l), values.T * keep_rl, hot_at_l)
        in_r = spread(table_place(row_l, device_r), values * keep_lr, hot_at_r)
        ours = pack_table(jnp.where(swapped, in_r, in_l))
        theirs = pack_table(jnp.where(swapped, in_l, in_r))
        gl_ref[:, feat:] = ours
        gr_ref[:, feat:] = jnp.concatenate([theirs[rs:], theirs[:rs]], 1)
    else:
        across, within = values[:rs], values[rs:]
        low_part, high_part = jnp.where(lower, within, 0.0), jnp.where(upper, within, 0.0)
        val_ll = jnp.concatenate([jnp.concatenate([low_part + low_part.T, across], 1),
                                  jnp.concatenate([across.T, high_part + high_part.T], 1)], 0)
        val_ll = jnp.where(eye, kself[:, :gs], val_ll) * keep_ll
        rows = jnp.where(diag, table_place(row_l, device_l),
                         jnp.concatenate([table_place(row_r, device_l)] * 2, 0))
        vals = jnp.where(diag, val_ll, jnp.concatenate([values.T * keep_rl, jnp.zeros((rs, gs), F32)], 0))
        ours = pack_table(spread(rows, vals, hot_at_l))
        theirs = pack_table(jnp.where(diag, 0.0, spread(table_place(row_l, device_r), values * keep_lr, hot_at_r)))
        gl_ref[:, feat:] = ours + before_l_ref[:, feat:]
        gr_ref[:, feat:] = theirs[:rs]
        rest_ref[...] = theirs[rs:]


def pair_kernel(call, mode, packets, dims, before=()):
    gs, npos, side, col_count, per_row, part = dims
    cols = side // SUBS
    tiles = gs * gs // 2 // LANES
    terms = LAYERS + CHAN
    field = (cols, side + 2, SUBS, LANES)
    feat = CHAN * npos
    tile_rows = 2 * gs // per_row
    lines = 4 * tile_rows * per_row * tile_rows // (per_row * part)
    rs = gs // 2
    shapes = [(gs, feat + lines)] + ([(rs, feat + 2 * lines), (rs, feat)] if call == 0 else [(rs, feat + lines), (rs, lines)])
    vm = pl.BlockSpec(memory_space=pltpu.VMEM)
    operands = (mode, *packets, *before)
    return pl.pallas_call(
        functools.partial(kernel_body, dims, call),
        out_shape=[jax.ShapeDtypeStruct(shape, F32) for shape in shapes],
        in_specs=[pl.BlockSpec(memory_space=pltpu.SMEM)] + [vm] * (len(operands) - 1),
        out_specs=[vm] * len(shapes),
        scratch_shapes=[
            pltpu.VMEM((CHAN, 2 * gs, npos), F32),
            pltpu.VMEM((LAYERS,) + field, F32),
            pltpu.VMEM((LAYERS, cols, side, SUBS, LANES), F32),
            pltpu.VMEM((LAYERS, 2 * gs, npos), F32),
            pltpu.VMEM((2,) + field, F32),
            pltpu.VMEM((LAYERS,) + field, F32),
            pltpu.VMEM((LAYERS,) + field, F32),
            pltpu.VMEM((terms, 2 * gs, npos), F32),
            pltpu.VMEM((tiles, terms, rs, SUBS, npos), F32),
            pltpu.VMEM((tiles, 1, LANES), F32),
            pltpu.VMEM((tiles, 1, LANES), F32),
        ],
        compiler_params=pltpu.CompilerParams(vmem_limit_bytes=40 * 1024 * 1024),
        cost_estimate=pl.CostEstimate(flops=2 * 10**10, bytes_accessed=5 * 10**7, transcendentals=10**6),
        name="pair_fields",
    )(*operands)


def exchange(x, rows, cols, target):
    perm = []
    for r in range(rows):
        for c in range(cols):
            tr, tc = target(r, c)
            perm.append((r * cols + c, tr * cols + tc))
    return lax.ppermute(x, ("row", "col"), perm)


def body(images, cotangent):
    rows = lax.axis_size("row")
    cols = lax.axis_size("col")
    row = lax.axis_index("row")
    col = lax.axis_index("col")
    per_row, _, part, feat = images.shape
    members = rows // 2
    groups = 2 * cols
    assert members == cols and members & (members - 1) == 0
    tile_rows = part * rows
    last = members // 2
    npos = feat // CHAN
    side = math.isqrt(npos)
    count = per_row * part
    gs = members * count
    own = images.reshape(count * CHAN, SUBS, npos // SUBS).transpose(0, 2, 1).reshape(count, feat)

    def partner_of(r, c, flip=0, turn=0):
        half, m = r // members, r % members
        step = m // last * (2 * m + 1 - members) + (1 - m // last) * (2 * m + 2)
        other = (half * cols + c + step) % groups
        return (other // cols ^ turn) * members + (m ^ flip), other % cols

    holders = {}
    for r in range(rows):
        for c in range(cols):
            holders[partner_of(r, c)] = (r, c)

    def holder_of(r, c, flip=0, turn=0):
        return holders[r ^ flip ^ turn * members, c]

    def swap(x, bit):
        return exchange(x, rows, cols, lambda r, c: (r ^ bit, c))

    cot_own = cotangent.reshape(count // 2, -1)
    packet = jnp.concatenate([own, jnp.concatenate([cot_own, swap(cot_own, members)], 0)], 1)
    bits = []
    while 1 << len(bits) < members:
        bits.append(1 << len(bits))
    near = packet
    for bit in bits[:-1]:
        near = jnp.concatenate([near, swap(near, bit)], 0)
    packets = [near, swap(near, last)]
    packets += [exchange(near, rows, cols, functools.partial(holder_of, flip=f)) for f in (0, last)]
    p_row, p_col = partner_of(row, col)
    member = row % members
    half = row // members
    flag = member == last - 1
    mode = jnp.stack([flag.astype(jnp.int32), member, col, half, p_col, p_row // members, row, p_row])
    mode = mode.astype(jnp.int32)

    dims = (gs, npos, side, cols, per_row, part)
    half_count = gs // 2
    gl, gr, rest = pair_kernel(0, mode, packets, dims)
    first = exchange(gr, rows, cols, partner_of)
    gl, gr, rest = pair_kernel(1, mode, packets, dims, before=(gl, rest))
    lines = rest.shape[1]
    gr = exchange(gr, rows, cols, partner_of)
    rest = exchange(rest, rows, cols, functools.partial(partner_of, flip=last))
    met = swap(gl[half_count:] + first[:, :feat + lines], last)
    out = gl[:half_count] + met + gr + jnp.pad(first[:, feat + lines:] + rest, ((0, 0), (feat, 0)))
    for bit in bits[-2::-1]:
        n = out.shape[0] // 2
        out = out[:n] + swap(out[n:], bit)
    table = out[:, feat:]
    n = lines // 2
    table = table[:, :n] + swap(table[:, n:], members)
    width = per_row * tile_rows
    table = table.reshape(count, n // width, width).transpose(1, 0, 2)
    grads = out[:, :feat].reshape(count * CHAN, npos // SUBS, SUBS).transpose(0, 2, 1)
    return (table.reshape(2, tile_rows, per_row, 1, tile_rows),
            grads.reshape(per_row, 1, part, feat))


def solution(mesh):
    return jax.shard_map(
        body,
        mesh=mesh,
        in_specs=(P(None, "col", "row", None), P("row", None, None, "col", None)),
        out_specs=(P("row", None, None, "col", None), P(None, "col", "row", None)),
        check_vma=False,
    )
```

```python
import functools, math
import jax, jax.numpy as jnp, numpy as np
from jax import lax
from jax.experimental import pallas as pl
from jax.experimental.pallas import tpu as pltpu
from jax.sharding import PartitionSpec as P

CHAN = 3
LAYERS = 3
WEIGHT_VAR = 2.0
BIAS_VAR = 0.1
LANES = 128
SUBS = 8
TINY = 1e-30
F32 = jnp.float32


def arccos_coefficients(degree):
    nodes = 0.5 + 0.5 * np.cos(np.pi * (np.arange(400) + 0.5) / 400)
    target = np.arccos(1.0 - nodes) / np.sqrt(nodes)
    fit = np.polynomial.chebyshev.Chebyshev.fit(nodes, target, degree, domain=[0.0, 1.0])
    return [float(c) for c in fit.convert(kind=np.polynomial.Polynomial).coef]


COEFFS = arccos_coefficients(5)


def row_sums(ref, v, cols):
    f = [ref[j, v] for j in range(cols)]
    sub = lax.broadcasted_iota(jnp.int32, (SUBS, LANES), 0)
    above = jnp.where(sub > 0, pltpu.roll(f[-1], 1, 0), 0.0)
    below = jnp.where(sub < SUBS - 1, pltpu.roll(f[0], SUBS - 1, 0), 0.0)
    g = [above] + f + [below]
    out = []
    for j in range(0, cols, 2):
        mid = g[j + 1] + g[j + 2]
        out.append(g[j] + mid)
        out.append(mid + g[j + 3])
    return out


def sweep(ref, side, cols, emit, carry=(), chunk=32):
    def body(i, state):
        prev, cur, extra = state
        base = i * chunk
        for o in range(0, chunk, 2):
            nxt = row_sums(ref, base + o + 2, cols)
            nxt2 = row_sums(ref, base + o + 3, cols)
            mid = [a + b for a, b in zip(cur, nxt)]
            extra = emit(base + o, [a + b for a, b in zip(prev, mid)], extra)
            extra = emit(base + o + 1, [a + b for a, b in zip(mid, nxt2)], extra)
            prev, cur = nxt, nxt2
        return prev, cur, extra

    zero = [jnp.zeros((SUBS, LANES), F32) for _ in range(cols)]
    first = row_sums(ref, 1, cols)
    return lax.fori_loop(0, side // chunk, body, (zero, first, carry))[2]


def one_hot(index, count):
    return (lax.broadcasted_iota(jnp.int32, (index.shape[0], count), 1) == index).astype(F32)


def pick(hot, values, dims):
    high = values.astype(jnp.bfloat16)
    rest = values - high.astype(F32)
    mid = rest.astype(jnp.bfloat16)
    low = (rest - mid.astype(F32)).astype(jnp.bfloat16)
    hot = hot.astype(jnp.bfloat16)
    (left,), (right,) = dims
    return lax.dot_general(jnp.concatenate([hot] * 3, left), jnp.concatenate([high, mid, low], right),
                           (dims, ((), ())), preferred_element_type=F32)


def fold_rows(tiles):
    sub = lax.broadcasted_iota(jnp.int32, (SUBS, LANES), 0)
    shift = SUBS // 2
    while shift:
        low = sub // shift % 2 == 0
        count = len(tiles) // 2
        tiles = [jnp.where(low, x + pltpu.roll(x, SUBS - shift, 0), y + pltpu.roll(y, shift, 0))
                 for x, y in zip(tiles[:count], tiles[count:])]
        shift //= 2
    return tiles[0]


def kernel_body(dims, call, *refs):
    gs, npos, side, col_count, per_row, part = dims
    mode_ref, a_refs, b_refs = refs[0], refs[1:3], refs[3:5]
    refs = refs[5:]
    if call == 1:
        before_l_ref, before_r_ref = refs[:2]
        refs = refs[2:]
    gl_ref, gr_ref, rest_ref = refs[:3]
    x_ref, v_ref, kb_ref, sg_ref, f_ref, phi_ref, sin_ref, d_ref, r_ref, w_ref, kv_ref = refs[3:]
    feat = CHAN * npos
    own_count = per_row * part
    members = gs // own_count
    tile_rows = 2 * members * part
    rows_of_dev = 2 * tile_rows
    width = per_row * tile_rows
    total_rows = 2 * members * rows_of_dev
    rs = gs // 2
    two = 2 * gs
    cols = side // SUBS
    tiles = gs * rs // LANES
    apt = LANES // rs
    blocks = npos // LANES
    per = LANES // SUBS
    flag = mode_ref[0] == 1
    diag = flag if call == 1 else None
    swapped = jnp.logical_and(flag, mode_ref[3] == 1)
    member = mode_ref[1]
    own_row, their_row = mode_ref[6], mode_ref[7]
    lane = lax.broadcasted_iota(jnp.int32, (SUBS, LANES), 1)
    sub = lax.broadcasted_iota(jnp.int32, (SUBS, LANES), 0)

    def col_of(tile):
        return tile // side, tile % side + 1

    def places(col, half, axis, first, count):
        shape = (count, 1) if axis == 0 else (1, count)
        i = lax.broadcasted_iota(jnp.int32, shape, axis) + first
        k = i // part % per_row
        idx = (half * members + jnp.bitwise_xor(member, i // own_count)) * part + i % part
        blk = k * col_count + col
        return blk, blk * tile_rows + idx, k * tile_rows + idx

    def table_place(at_row, device):
        apart = jnp.bitwise_xor(at_row // rows_of_dev, device)
        return (apart % members * 2 + apart // members) * rows_of_dev + at_row % rows_of_dev

    def pack_table(rows):
        lines = []
        for q in range(rows.shape[0] // (2 * rows_of_dev)):
            first = q * 2 * rows_of_dev
            lines.append(jnp.concatenate([rows[first + t:first + t + own_count]
                                          for t in range(0, 2 * rows_of_dev, own_count)], 1))
        return jnp.concatenate(lines, 0)

    per_line = (a_refs[0].shape[1] - feat) // width

    def packet_place(at_row, device):
        apart = jnp.bitwise_xor(at_row // rows_of_dev, device)
        within = at_row % rows_of_dev
        line = apart % members * own_count + apart // members * (own_count // 2) + within // per_line
        return within % per_line * gs + line

    def packet_table(packets):
        rows = jnp.concatenate([ref[:, feat:].astype(F32) for ref in packets], 0)
        return jnp.concatenate([rows[:, i * width:(i + 1) * width] for i in range(per_line)], 0).astype(jnp.bfloat16)

    ours_at = (mode_ref[2], mode_ref[3], own_row)
    theirs_at = (mode_ref[4], mode_ref[5], their_row)
    ca = packet_table(a_refs)
    cb = packet_table(b_refs)
    if call == 0:
        col_l, half_l, device_l = [jnp.where(swapped, t, o) for o, t in zip(ours_at, theirs_at)]
        col_r, half_r, device_r = [jnp.where(swapped, o, t) for o, t in zip(ours_at, theirs_at)]
        first_r = jnp.where(swapped, 0, rs)
        table_l, table_r = jnp.where(swapped, cb, ca), jnp.where(swapped, ca, cb)
    else:
        (col_l, half_l, device_l), (col_r, half_r, device_r) = ours_at, theirs_at
        first_r = 0
        table_l, table_r = ca, cb
    blk_l, row_l, at_l = places(col_l, half_l, 0, 0, gs)
    blk_ll = places(col_l, half_l, 1, 0, gs)[0]
    blk_r, row_r, at_r = places(col_r, half_r, 0, first_r, rs)
    blk_rl = places(col_r, half_r, 1, first_r, rs)[0]
    hot_at_l, hot_at_r = one_hot(at_l, width), one_hot(at_r, width)
    keep_lr = (blk_l <= blk_rl).astype(F32)
    keep_rl = (blk_r <= blk_ll).astype(F32)

    def chosen(rows, table, columns):
        picked = jnp.dot(one_hot(rows, total_rows).astype(jnp.bfloat16), table.astype(jnp.bfloat16),
                         preferred_element_type=F32)
        return lax.dot_general(picked.astype(jnp.bfloat16), columns.astype(jnp.bfloat16),
                               (((1,), (1,)), ((), ())), preferred_element_type=F32)
    w_all = (chosen(packet_place(row_l, device_r), table_r, hot_at_r) * keep_lr
             + (chosen(packet_place(row_r, device_l), table_l, hot_at_l) * keep_rl).T)
    if call == 1:
        keep_ll = (blk_l <= blk_ll).astype(F32)
        w_ll = chosen(packet_place(row_l, device_l), table_l, hot_at_l) * keep_ll
        w_sym = w_ll + w_ll.T
        eye = (lax.broadcasted_iota(jnp.int32, (gs, gs), 0) == lax.broadcasted_iota(jnp.int32, (gs, gs), 1))
        half_row = lax.broadcasted_iota(jnp.int32, (rs, rs), 0)
        half_col = lax.broadcasted_iota(jnp.int32, (rs, rs), 1)
        upper, lower = half_row < half_col, half_row > half_col
        w_diag = jnp.concatenate(
            [w_sym[:rs, rs:], jnp.where(upper, w_sym[rs:, rs:], jnp.where(lower, w_sym[:rs, :rs], 0.0))], 0)
        w_all = jnp.where(diag, w_diag, w_all)
        self_l = jnp.sum(jnp.where(eye, w_ll, 0.0), 0, keepdims=True)
        self_row = jnp.concatenate([self_l, jnp.zeros((1, LANES - gs), F32)], 1)
        self_row = jnp.where(diag, self_row, 0.0)
    tile_hot = one_hot(lax.broadcasted_iota(jnp.int32, (gs, 1), 0) // apt, tiles)
    lane_hot = (lax.broadcasted_iota(jnp.int32, (rs, LANES), 1) // apt
                == lax.broadcasted_iota(jnp.int32, (rs, LANES), 0)).astype(F32)
    lane_match = (lax.broadcasted_iota(jnp.int32, (gs, LANES), 1) % apt
                  == lax.broadcasted_iota(jnp.int32, (gs, LANES), 0) % apt)
    w_lanes = jnp.where(lane_match, pick(lane_hot.T, w_all.T, ((1,), (0,))).T, 0.0)
    w_rows = pick(tile_hot.T, w_lanes, ((1,), (0,)))
    for k in range(tiles):
        w_ref[k] = w_rows[k:k + 1]
    zeros = jnp.zeros((SUBS, LANES), F32)
    def image_rows(sl):
        a = [ref[:, sl].astype(F32) for ref in a_refs]
        if call == 0:
            b = [ref[:, sl].astype(F32) for ref in b_refs]
            left = jnp.where(swapped, jnp.concatenate(b, 0), jnp.concatenate(a, 0))
            right = jnp.where(swapped, a[0], b[1])
        else:
            left = jnp.concatenate(a, 0)
            right = jnp.where(diag, a[1], b_refs[0][:, sl].astype(F32))
        return jnp.concatenate([left, right, jnp.zeros((two - gs - rs, LANES), F32)], 0)

    def to_fields(x, store):
        t = jnp.concatenate([x, x], 0).T
        return [store(i, t[i * SUBS:(i + 1) * SUBS]) for i in range(per)]

    for blk in range(blocks):
        total = 0.0
        for ch in range(CHAN):
            x = image_rows(pl.ds(ch * npos + blk * LANES, LANES))
            x_ref[ch, :, pl.ds(blk * LANES, LANES)] = x
            total = total + x * x

        def store(i, t):
            j, v = col_of(blk * per + i)
            f_ref[0, j, v] = t
        to_fields(total * (1.0 / CHAN), store)
    for j in range(cols):
        for v in (0, side + 1):
            for l in range(LAYERS):
                v_ref[l, j, v] = zeros
                phi_ref[l, j, v] = zeros
            f_ref[0, j, v] = zeros
            f_ref[1, j, v] = zeros

    def block_of(ref_at, blk):
        vals = []
        for t in range(per):
            j, v = col_of(blk * per + t)
            vals.append(ref_at(j, v))
        return jnp.concatenate(vals, 0)

    inner = WEIGHT_VAR / (9.0 * 2.0 * math.pi)
    scales = [WEIGHT_VAR / (9.0 * CHAN)]
    while len(scales) < LAYERS:
        scales.append(scales[-1] * inner)

    def var_emit(l, scale):
        def emit(v, sums, extra):
            for j in range(cols):
                v_ref[l, j, v + 1] = sums[j] * (scale / scales[l]) + BIAS_VAR / scales[l]
            return extra
        return emit
    sweep(f_ref.at[0], side, cols, var_emit(0, WEIGHT_VAR / 9.0))
    for l in range(1, LAYERS):
        sweep(v_ref.at[l - 1], side, cols, var_emit(l, 0.5 * WEIGHT_VAR / 9.0 * scales[l - 1]))
    for l in range(LAYERS):
        for blk in range(blocks):
            t = block_of(lambda j, v: v_ref[l, j, v], blk).T[:two]
            sg_ref[l, :, pl.ds(blk * LANES, LANES)] = t * lax.rsqrt(t)
    totals = [zeros] * cols
    for j in range(cols):
        for v in range(side):
            totals[j] = totals[j] + v_ref[LAYERS - 1, j, v + 1]
    kself = jnp.sum(sum(totals), 0, keepdims=True) * (0.5 * WEIGHT_VAR / npos * scales[-1]) + BIAS_VAR

    def clear(i, _):
        sl = pl.ds(pl.multiple_of(i * LANES, LANES), LANES)
        d_ref[:, :, sl] = jnp.zeros((LAYERS + CHAN, two, LANES), F32)
        return 0
    lax.fori_loop(0, blocks, clear, 0)

    def pair_tile(k, _):
        a0 = pl.multiple_of(k * apt, SUBS)
        masked = jnp.logical_and(diag, a0 >= rs) if call == 1 else False
        lo0 = pl.multiple_of(jnp.maximum(a0 - rs, 0), SUBS)

        def put(blk, t):
            half = blk * per
            j = half // side
            v = half % side + 1
            for i in range(per):
                f_ref[0, j, v + i] = t[i * SUBS:(i + 1) * SUBS]

        def cross_plain(blk, _):
            sl = pl.ds(pl.multiple_of(blk * LANES, LANES), LANES)
            rows = []
            left = [x_ref[ch, pl.ds(a0, SUBS), sl] for ch in range(CHAN)]
            for b in range(rs):
                acc = left[0] * x_ref[0, gs + b:gs + b + 1, sl]
                for ch in range(1, CHAN):
                    acc = acc + left[ch] * x_ref[ch, gs + b:gs + b + 1, sl]
                rows.append(acc)
            put(blk, jnp.concatenate(rows, 0).T)
            return 0

        def cross_masked(blk, _):
            sl = pl.ds(pl.multiple_of(blk * LANES, LANES), LANES)
            rows = []
            left = [x_ref[ch, pl.ds(a0, SUBS), sl] for ch in range(CHAN)]
            low = [x_ref[ch, pl.ds(lo0, SUBS), sl] for ch in range(CHAN)]
            for b in range(rs):
                first = sub + lo0 < b
                acc = 0.0
                for ch in range(CHAN):
                    acc = acc + jnp.where(first, left[ch] * x_ref[ch, gs + b:gs + b + 1, sl],
                                          low[ch] * x_ref[ch, b:b + 1, sl])
                rows.append(acc)
            put(blk, jnp.concatenate(rows, 0).T)
            return 0

        def either(plain, with_mask):
            if call == 0:
                plain()
                return

            @pl.when(jnp.logical_not(masked))
            def _():
                plain()

            @pl.when(masked)
            def _():
                with_mask()

        either(lambda: lax.fori_loop(0, blocks, cross_plain, 0, unroll=True),
               lambda: lax.fori_loop(0, blocks, cross_masked, 0, unroll=True))

        ia, ib = lane % apt, lane // apt
        il, ir = ia + a0, ib + gs
        if call == 1:
            second = jnp.logical_and(masked, ib <= lo0 + ia)
            il = jnp.where(second, ia + lo0, il)
            ir = jnp.where(second, ib, ir)

        @pl.when(jnp.logical_or(k == 0, masked) if call == 1 else k == 0)
        def _():
            def gather(v, _):
                for l in range(LAYERS):
                    for j in range(cols):
                        kb_ref[l, j, v] = jnp.take_along_axis(v_ref[l, j, v + 1], ir, axis=1)
                return 0
            lax.fori_loop(0, side, gather, 0, unroll=True)

        parity = k % 2

        def relu_emit(l, dst):
            def emit(v, sums, extra):
                for j in range(cols):
                    k12 = sums[j] + BIAS_VAR / scales[l]
                    prod = jnp.take_along_axis(v_ref[l, j, v + 1], il, axis=1) * kb_ref[l, j, v]
                    inv = lax.rsqrt(prod)
                    cosine = k12 * inv
                    w = jnp.maximum(1.0 - jnp.abs(cosine), TINY)
                    poly = COEFFS[-1]
                    for c in COEFFS[-2::-1]:
                        poly = poly * w + c
                    angle = (w * lax.rsqrt(w)) * poly
                    phi = jnp.where(cosine >= 0.0, math.pi - angle, angle)
                    rest = jnp.maximum(prod - k12 * k12, TINY)
                    root = rest * lax.rsqrt(rest)
                    value = root + phi * k12
                    phi_ref[l, j, v + 1] = phi
                    sin_ref[parity, l, j, v + 1] = root * inv
                    if dst is None:
                        extra = extra + value
                    else:
                        f_ref[dst, j, v + 1] = value
                return extra
            return emit

        sweep(f_ref.at[0], side, cols, relu_emit(0, 1))
        sweep(f_ref.at[1], side, cols, relu_emit(1, 0))
        total = sweep(f_ref.at[0], side, cols, relu_emit(2, None), zeros)
        kv_ref[k] = jnp.sum(total, 0, keepdims=True) * (WEIGHT_VAR / (2.0 * math.pi * npos) * scales[-1]) + BIAS_VAR

        wrow = jnp.broadcast_to(w_ref[k] * (WEIGHT_VAR / npos), (SUBS, LANES))
        wscaled = wrow * inner

        def back_emit(l, dst, scaled):
            def emit(v, sums, extra):
                for j in range(cols):
                    grad = sums[j] * wscaled if scaled else sums[j]
                    sin_ref[parity, l, j, v + 1] = sin_ref[parity, l, j, v + 1] * grad
                    f_ref[dst, j, v + 1] = phi_ref[l, j, v + 1] * grad
                return extra
            return emit
        sweep(phi_ref.at[2], side, cols, back_emit(1, 0, True))
        sweep(f_ref.at[0], side, cols, back_emit(0, 1, False))

        def last_emit(v, sums, extra):
            for j in range(cols):
                sin_ref[parity, LAYERS, j, v + 1] = sums[j]
            return extra
        sweep(f_ref.at[1], side, cols, last_emit)

        starts = [pl.multiple_of(a0 - apt, SUBS), a0]
        lows = [pl.multiple_of(jnp.maximum(a0 - apt - rs, 0), SUBS), lo0]
        wrows = [jnp.broadcast_to(w_ref[jnp.maximum(k - 1, 0)] * (WEIGHT_VAR / npos), (SUBS, LANES)), wrow]

        def fold(is_masked):
            def body(blk, _):
                sl = pl.ds(pl.multiple_of(blk * LANES, LANES), LANES)
                half = blk * per
                j = half // side
                v = half % side + 1

                def turned(t, l):
                    rows = [sin_ref[t, l, j, v + i] for i in range(per)]
                    if l == LAYERS - 1:
                        rows = [row * wrows[t] for row in rows]
                    h = jnp.concatenate(rows, 0).T
                    return [h[b * SUBS:(b + 1) * SUBS] for b in range(rs)]

                for l in range(LAYERS + 1):
                    h = [turned(t, l) for t in range(2)]
                    terms = [(l, sg_ref, l)] if l < LAYERS else [(LAYERS + ch, x_ref, ch) for ch in range(CHAN)]
                    for slot, src, at in terms:
                        left = [src[at, pl.ds(start, SUBS), sl] for start in starts]
                        totals = [0.0, 0.0]
                        if is_masked:
                            for t in range(2):
                                i = sub + t * apt
                                low = src[at, pl.ds(lows[t], SUBS), sl]
                                low_total = 0.0
                                for b in range(rs):
                                    terms_b = []
                                    if b > t * apt:
                                        first = h[t][b] if b >= (t + 1) * apt else jnp.where(i < b, h[t][b], 0.0)
                                        totals[t] = totals[t] + first * src[at, gs + b:gs + b + 1, sl]
                                        terms_b.append(first * left[t])
                                    if b < (t + 1) * apt - 1:
                                        other = h[t][b] if b < t * apt else jnp.where(i > b, h[t][b], 0.0)
                                        low_total = low_total + other * src[at, b:b + 1, sl]
                                        terms_b.append(other * low)
                                    r_ref[1 + t, slot, b, :, sl] = sum(terms_b)
                                at_rows = pl.ds(lows[t], SUBS)
                                d_ref[slot, at_rows, sl] = d_ref[slot, at_rows, sl] + low_total
                        else:
                            for b in range(rs):
                                right = src[at, gs + b:gs + b + 1, sl]
                                for t in range(2):
                                    totals[t] = totals[t] + h[t][b] * right
                                r_ref[k // 2, slot, b, :, sl] = h[0][b] * left[0] + h[1][b] * left[1]
                        for t in range(2):
                            at_rows = pl.ds(starts[t], SUBS)
                            d_ref[slot, at_rows, sl] = d_ref[slot, at_rows, sl] + totals[t]
                return 0
            lax.fori_loop(0, blocks, body, 0, unroll=True)

        @pl.when(parity == 1)
        def _():
            either(lambda: fold(False), lambda: fold(True))
        return 0

    lax.fori_loop(0, tiles, pair_tile, 0)

    def gather_right(low):
        def body(blk, _):
            sl = pl.ds(pl.multiple_of(blk * LANES, LANES), LANES)
            for slot in range(LAYERS + CHAN):
                for b0 in range(0, rs, SUBS):
                    sums = []
                    for b in range(b0, b0 + SUBS):
                        if low is None:
                            t = r_ref[0, slot, b, :, sl] + r_ref[1, slot, b, :, sl]
                        else:
                            t = 0.0 if low else r_ref[0, slot, b, :, sl]
                            for n in range(2):
                                part = r_ref[1 + n, slot, b, :, sl]
                                if n * apt <= b < (n + 1) * apt:
                                    i = sub + n * apt
                                    t = t + jnp.where(i > b if low else i < b, part, 0.0)
                                elif (b < n * apt) == bool(low):
                                    t = t + part
                        sums.append(t)
                    at = pl.ds(b0 if low else gs + b0, SUBS)
                    d_ref[slot, at, sl] = d_ref[slot, at, sl] + fold_rows(sums)
            return 0
        lax.fori_loop(0, blocks, body, 0, unroll=True)

    if call == 0:
        gather_right(None)
    else:
        @pl.when(jnp.logical_not(diag))
        def _():
            gather_right(None)

        @pl.when(diag)
        def _():
            gather_right(0)
            gather_right(1)

    selfw = self_row * (0.5 * WEIGHT_VAR / npos) if call == 1 else 0.0
    for l in range(LAYERS):
        dest = phi_ref if l == LAYERS - 1 else sin_ref.at[0]
        scale = (inner if l == 0 else 1.0) / (4.0 * math.pi)
        for blk in range(blocks):
            def store(i, t):
                j, v = col_of(blk * per + i)
                t = t * (lax.rsqrt(v_ref[l, j, v]) * scale)
                dest[l, j, v] = t + selfw if l == LAYERS - 1 else t
            to_fields(d_ref[l, :, pl.ds(blk * LANES, LANES)], store)

    def chain_emit(l):
        def emit(v, sums, extra):
            for j in range(cols):
                phi_ref[l, j, v + 1] = sin_ref[0, l, j, v + 1] + sums[j] * (0.5 * WEIGHT_VAR / 9.0)
            return extra
        return emit
    sweep(phi_ref.at[2], side, cols, chain_emit(1))
    sweep(phi_ref.at[1], side, cols, chain_emit(0))

    def final_emit(v, sums, extra):
        for j in range(cols):
            f_ref[0, j, v + 1] = sums[j] * (WEIGHT_VAR / 9.0 * 2.0 / CHAN)
        return extra
    sweep(phi_ref.at[0], side, cols, final_emit)
    for blk in range(blocks):
        e = block_of(lambda j, v: f_ref[0, j, v], blk).T[:two]
        at = pl.ds(blk * LANES, LANES)
        for ch in range(CHAN):
            sl = pl.ds(ch * npos + blk * LANES, LANES)
            grad = d_ref[LAYERS + ch, :, at] * (inner * inner / CHAN) + x_ref[ch, :, at] * e
            left, right = grad[:gs], grad[gs:gs + rs]
            if call == 0:
                near = jnp.where(swapped, right, left[:rs])
                gl_ref[:, sl] = jnp.concatenate([near, jnp.where(swapped, 0.0, left[rs:])], 0)
                gr_ref[:, sl] = jnp.where(swapped, left[rs:], right)
                rest_ref[:, sl] = jnp.where(swapped, left[:rs], 0.0)
            else:
                far = left[rs:] + jnp.where(diag, right, 0.0)
                gl_ref[:, sl] = jnp.concatenate([left[:rs], far], 0) + before_l_ref[:, sl]
                gr_ref[:, sl] = jnp.where(diag, before_r_ref[:, sl], right)

    kv = jnp.concatenate([kv_ref[k] for k in range(tiles)], 0)
    values = pick(lane_hot, jnp.where(lane_match, pick(tile_hot, kv, ((1,), (0,))), 0.0).T, ((1,), (0,))).T

    def spread(rows, vals, columns):
        placed = pick(columns.T, vals.T, ((1,), (0,))).T
        return pick(one_hot(rows, total_rows).T, placed, ((1,), (0,)))
    if call == 0:
        in_l = spread(table_place(row_r, device_l), values.T * keep_rl, hot_at_l)
        in_r = spread(table_place(row_l, device_r), values * keep_lr, hot_at_r)
        ours = pack_table(jnp.where(swapped, in_r, in_l))
        theirs = pack_table(jnp.where(swapped, in_l, in_r))
        gl_ref[:, feat:] = ours
        gr_ref[:, feat:] = jnp.concatenate([theirs[rs:], theirs[:rs]], 1)
    else:
        across, within = values[:rs], values[rs:]
        low_part, high_part = jnp.where(lower, within, 0.0), jnp.where(upper, within, 0.0)
        val_ll = jnp.concatenate([jnp.concatenate([low_part + low_part.T, across], 1),
                                  jnp.concatenate([across.T, high_part + high_part.T], 1)], 0)
        val_ll = jnp.where(eye, kself[:, :gs], val_ll) * keep_ll
        rows = jnp.where(diag, table_place(row_l, device_l),
                         jnp.concatenate([table_place(row_r, device_l)] * 2, 0))
        vals = jnp.where(diag, val_ll, jnp.concatenate([values.T * keep_rl, jnp.zeros((rs, gs), F32)], 0))
        ours = pack_table(spread(rows, vals, hot_at_l))
        theirs = pack_table(jnp.where(diag, 0.0, spread(table_place(row_l, device_r), values * keep_lr, hot_at_r)))
        gl_ref[:, feat:] = ours + before_l_ref[:, feat:]
        gr_ref[:, feat:] = theirs[:rs]
        rest_ref[...] = theirs[rs:]


def pair_kernel(call, mode, packets, dims, before=()):
    gs, npos, side, col_count, per_row, part = dims
    cols = side // SUBS
    tiles = gs * gs // 2 // LANES
    terms = LAYERS + CHAN
    field = (cols, side + 2, SUBS, LANES)
    feat = CHAN * npos
    tile_rows = 2 * gs // per_row
    lines = 4 * tile_rows * per_row * tile_rows // (per_row * part)
    rs = gs // 2
    shapes = [(gs, feat + lines)] + ([(rs, feat + 2 * lines), (rs, feat)] if call == 0 else [(rs, feat + lines), (rs, lines)])
    vm = pl.BlockSpec(memory_space=pltpu.VMEM)
    operands = (mode, *packets, *before)
    return pl.pallas_call(
        functools.partial(kernel_body, dims, call),
        out_shape=[jax.ShapeDtypeStruct(shape, F32) for shape in shapes],
        in_specs=[pl.BlockSpec(memory_space=pltpu.SMEM)] + [vm] * (len(operands) - 1),
        out_specs=[vm] * len(shapes),
        scratch_shapes=[
            pltpu.VMEM((CHAN, 2 * gs, npos), F32),
            pltpu.VMEM((LAYERS,) + field, F32),
            pltpu.VMEM((LAYERS, cols, side, SUBS, LANES), F32),
            pltpu.VMEM((LAYERS, 2 * gs, npos), F32),
            pltpu.VMEM((2,) + field, F32),
            pltpu.VMEM((LAYERS,) + field, F32),
            pltpu.VMEM((2, LAYERS + 1) + field, F32),
            pltpu.VMEM((terms, 2 * gs, npos), F32),
            pltpu.VMEM((3, terms, rs, SUBS, npos), F32),
            pltpu.VMEM((tiles, 1, LANES), F32),
            pltpu.VMEM((tiles, 1, LANES), F32),
        ],
        compiler_params=pltpu.CompilerParams(vmem_limit_bytes=40 * 1024 * 1024),
        cost_estimate=pl.CostEstimate(flops=2 * 10**10, bytes_accessed=5 * 10**7, transcendentals=10**6),
        name="pair_fields",
    )(*operands)


def exchange(x, rows, cols, target):
    perm = []
    for r in range(rows):
        for c in range(cols):
            tr, tc = target(r, c)
            perm.append((r * cols + c, tr * cols + tc))
    return lax.ppermute(x, ("row", "col"), perm)


def body(images, cotangent):
    rows = lax.axis_size("row")
    cols = lax.axis_size("col")
    row = lax.axis_index("row")
    col = lax.axis_index("col")
    per_row, _, part, feat = images.shape
    members = rows // 2
    groups = 2 * cols
    assert members == cols and members & (members - 1) == 0
    tile_rows = part * rows
    last = members // 2
    npos = feat // CHAN
    side = math.isqrt(npos)
    count = per_row * part
    gs = members * count
    own = images.reshape(count * CHAN, SUBS, npos // SUBS).transpose(0, 2, 1).reshape(count, feat)

    def partner_of(r, c, flip=0, turn=0):
        half, m = r // members, r % members
        step = m // last * (2 * m + 1 - members) + (1 - m // last) * (2 * m + 2)
        other = (half * cols + c + step) % groups
        return (other // cols ^ turn) * members + (m ^ flip), other % cols

    holders = {}
    for r in range(rows):
        for c in range(cols):
            holders[partner_of(r, c)] = (r, c)

    def holder_of(r, c, flip=0, turn=0):
        return holders[r ^ flip ^ turn * members, c]

    def swap(x, bit):
        return exchange(x, rows, cols, lambda r, c: (r ^ bit, c))

    cot_own = cotangent.reshape(count // 2, -1)
    packet = jnp.concatenate([own, jnp.concatenate([cot_own, swap(cot_own, members)], 0)], 1)
    bits = []
    while 1 << len(bits) < members:
        bits.append(1 << len(bits))
    near = packet
    for bit in bits[:-1]:
        near = jnp.concatenate([near, swap(near, bit)], 0)
    packets = [near, swap(near, last)]
    packets += [exchange(near, rows, cols, functools.partial(holder_of, flip=f)) for f in (0, last)]
    p_row, p_col = partner_of(row, col)
    member = row % members
    half = row // members
    flag = member == last - 1
    mode = jnp.stack([flag.astype(jnp.int32), member, col, half, p_col, p_row // members, row, p_row])
    mode = mode.astype(jnp.int32)

    dims = (gs, npos, side, cols, per_row, part)
    half_count = gs // 2
    gl, gr, rest = pair_kernel(0, mode, packets, dims)
    first = exchange(gr, rows, cols, partner_of)
    gl, gr, rest = pair_kernel(1, mode, packets, dims, before=(gl, rest))
    lines = rest.shape[1]
    gr = exchange(gr, rows, cols, partner_of)
    rest = exchange(rest, rows, cols, functools.partial(partner_of, flip=last))
    met = swap(gl[half_count:] + first[:, :feat + lines], last)
    out = gl[:half_count] + met + gr + jnp.pad(first[:, feat + lines:] + rest, ((0, 0), (feat, 0)))
    for bit in bits[-2::-1]:
        n = out.shape[0] // 2
        out = out[:n] + swap(out[n:], bit)
    table = out[:, feat:]
    n = lines // 2
    table = table[:, :n] + swap(table[:, n:], members)
    width = per_row * tile_rows
    table = table.reshape(count, n // width, width).transpose(1, 0, 2)
    grads = out[:, :feat].reshape(count * CHAN, npos // SUBS, SUBS).transpose(0, 2, 1)
    return (table.reshape(2, tile_rows, per_row, 1, tile_rows),
            grads.reshape(per_row, 1, part, feat))


def solution(mesh):
    return jax.shard_map(
        body,
        mesh=mesh,
        in_specs=(P(None, "col", "row", None), P("row", None, None, "col", None)),
        out_specs=(P("row", None, None, "col", None), P(None, "col", "row", None)),
        check_vma=False,
    )
```

```python
import functools, math
import jax, jax.numpy as jnp, numpy as np
from jax import lax
from jax.experimental import pallas as pl
from jax.experimental.pallas import tpu as pltpu
from jax.sharding import PartitionSpec as P

CHAN = 3
LAYERS = 3
WEIGHT_VAR = 2.0
BIAS_VAR = 0.1
LANES = 128
SUBS = 8
TINY = 1e-30
F32 = jnp.float32


def arccos_coefficients(degree):
    nodes = 0.5 + 0.5 * np.cos(np.pi * (np.arange(400) + 0.5) / 400)
    target = np.arccos(1.0 - nodes) / np.sqrt(nodes)
    fit = np.polynomial.chebyshev.Chebyshev.fit(nodes, target, degree, domain=[0.0, 1.0])
    return [float(c) for c in fit.convert(kind=np.polynomial.Polynomial).coef]


COEFFS = arccos_coefficients(5)


def row_sums(ref, v, cols):
    f = [ref[j, v] for j in range(cols)]
    sub = lax.broadcasted_iota(jnp.int32, (SUBS, LANES), 0)
    above = jnp.where(sub > 0, pltpu.roll(f[-1], 1, 0), 0.0)
    below = jnp.where(sub < SUBS - 1, pltpu.roll(f[0], SUBS - 1, 0), 0.0)
    g = [above] + f + [below]
    out = []
    for j in range(0, cols, 2):
        mid = g[j + 1] + g[j + 2]
        out.append(g[j] + mid)
        out.append(mid + g[j + 3])
    return out


def sweep(ref, side, cols, emit, carry=(), chunk=32):
    def body(i, state):
        prev, cur, extra = state
        base = i * chunk
        for o in range(0, chunk, 2):
            nxt = row_sums(ref, base + o + 2, cols)
            nxt2 = row_sums(ref, base + o + 3, cols)
            mid = [a + b for a, b in zip(cur, nxt)]
            extra = emit(base + o, [a + b for a, b in zip(prev, mid)], extra)
            extra = emit(base + o + 1, [a + b for a, b in zip(mid, nxt2)], extra)
            prev, cur = nxt, nxt2
        return prev, cur, extra

    zero = [jnp.zeros((SUBS, LANES), F32) for _ in range(cols)]
    first = row_sums(ref, 1, cols)
    return lax.fori_loop(0, side // chunk, body, (zero, first, carry))[2]


def one_hot(index, count):
    return (lax.broadcasted_iota(jnp.int32, (index.shape[0], count), 1) == index).astype(F32)


def pick(hot, values, dims):
    high = values.astype(jnp.bfloat16)
    rest = values - high.astype(F32)
    mid = rest.astype(jnp.bfloat16)
    low = (rest - mid.astype(F32)).astype(jnp.bfloat16)
    hot = hot.astype(jnp.bfloat16)
    (left,), (right,) = dims
    return lax.dot_general(jnp.concatenate([hot] * 3, left), jnp.concatenate([high, mid, low], right),
                           (dims, ((), ())), preferred_element_type=F32)


def fold_rows(tiles):
    sub = lax.broadcasted_iota(jnp.int32, (SUBS, LANES), 0)
    shift = SUBS // 2
    while shift:
        low = sub // shift % 2 == 0
        count = len(tiles) // 2
        tiles = [jnp.where(low, x + pltpu.roll(x, SUBS - shift, 0), y + pltpu.roll(y, shift, 0))
                 for x, y in zip(tiles[:count], tiles[count:])]
        shift //= 2
    return tiles[0]


def kernel_body(dims, call, *refs):
    gs, npos, side, col_count, per_row, part = dims
    mode_ref, a_refs, b_refs = refs[0], refs[1:3], refs[3:5]
    refs = refs[5:]
    if call == 1:
        before_l_ref, before_r_ref = refs[:2]
        refs = refs[2:]
    gl_ref, gr_ref, rest_ref = refs[:3]
    x_ref, v_ref, kb_ref, sg_ref, f_ref, phi_ref, sin_ref, d_ref, r_ref, w_ref, kv_ref = refs[3:]
    feat = CHAN * npos
    own_count = per_row * part
    members = gs // own_count
    tile_rows = 2 * members * part
    rows_of_dev = 2 * tile_rows
    width = per_row * tile_rows
    total_rows = 2 * members * rows_of_dev
    rs = gs // 2
    two = 2 * gs
    cols = side // SUBS
    tiles = gs * rs // LANES
    apt = LANES // rs
    blocks = npos // LANES
    per = LANES // SUBS
    flag = mode_ref[0] == 1
    diag = flag if call == 1 else None
    swapped = jnp.logical_and(flag, mode_ref[3] == 1)
    member = mode_ref[1]
    own_row, their_row = mode_ref[6], mode_ref[7]
    lane = lax.broadcasted_iota(jnp.int32, (SUBS, LANES), 1)
    sub = lax.broadcasted_iota(jnp.int32, (SUBS, LANES), 0)

    def col_of(tile):
        return tile // side, tile % side + 1

    def places(col, half, axis, first, count):
        shape = (count, 1) if axis == 0 else (1, count)
        i = lax.broadcasted_iota(jnp.int32, shape, axis) + first
        k = i // part % per_row
        idx = (half * members + jnp.bitwise_xor(member, i // own_count)) * part + i % part
        blk = k * col_count + col
        return blk, blk * tile_rows + idx, k * tile_rows + idx

    def table_place(at_row, device):
        apart = jnp.bitwise_xor(at_row // rows_of_dev, device)
        return (apart % members * 2 + apart // members) * rows_of_dev + at_row % rows_of_dev

    def pack_table(rows):
        lines = []
        for q in range(rows.shape[0] // (2 * rows_of_dev)):
            first = q * 2 * rows_of_dev
            lines.append(jnp.concatenate([rows[first + t:first + t + own_count]
                                          for t in range(0, 2 * rows_of_dev, own_count)], 1))
        return jnp.concatenate(lines, 0)

    per_line = (a_refs[0].shape[1] - feat) // width

    def packet_place(at_row, device):
        apart = jnp.bitwise_xor(at_row // rows_of_dev, device)
        within = at_row % rows_of_dev
        line = apart % members * own_count + apart // members * (own_count // 2) + within // per_line
        return within % per_line * gs + line

    def packet_table(packets):
        rows = jnp.concatenate([ref[:, feat:].astype(F32) for ref in packets], 0)
        return jnp.concatenate([rows[:, i * width:(i + 1) * width] for i in range(per_line)], 0).astype(jnp.bfloat16)

    ours_at = (mode_ref[2], mode_ref[3], own_row)
    theirs_at = (mode_ref[4], mode_ref[5], their_row)
    ca = packet_table(a_refs)
    cb = packet_table(b_refs)
    if call == 0:
        col_l, half_l, device_l = [jnp.where(swapped, t, o) for o, t in zip(ours_at, theirs_at)]
        col_r, half_r, device_r = [jnp.where(swapped, o, t) for o, t in zip(ours_at, theirs_at)]
        first_r = jnp.where(swapped, 0, rs)
        table_l, table_r = jnp.where(swapped, cb, ca), jnp.where(swapped, ca, cb)
    else:
        (col_l, half_l, device_l), (col_r, half_r, device_r) = ours_at, theirs_at
        first_r = 0
        table_l, table_r = ca, cb
    blk_l, row_l, at_l = places(col_l, half_l, 0, 0, gs)
    blk_ll = places(col_l, half_l, 1, 0, gs)[0]
    blk_r, row_r, at_r = places(col_r, half_r, 0, first_r, rs)
    blk_rl = places(col_r, half_r, 1, first_r, rs)[0]
    hot_at_l, hot_at_r = one_hot(at_l, width), one_hot(at_r, width)
    keep_lr = (blk_l <= blk_rl).astype(F32)
    keep_rl = (blk_r <= blk_ll).astype(F32)

    def chosen(rows, table, columns):
        picked = jnp.dot(one_hot(rows, total_rows).astype(jnp.bfloat16), table.astype(jnp.bfloat16),
                         preferred_element_type=F32)
        return lax.dot_general(picked.astype(jnp.bfloat16), columns.astype(jnp.bfloat16),
                               (((1,), (1,)), ((), ())), preferred_element_type=F32)
    tile_hot = one_hot(lax.broadcasted_iota(jnp.int32, (gs, 1), 0) // apt, tiles)
    lane_hot = (lax.broadcasted_iota(jnp.int32, (rs, LANES), 1) // apt
                == lax.broadcasted_iota(jnp.int32, (rs, LANES), 0)).astype(F32)
    lane_match = (lax.broadcasted_iota(jnp.int32, (gs, LANES), 1) % apt
                  == lax.broadcasted_iota(jnp.int32, (gs, LANES), 0) % apt)

    def set_weights(w_all):
        w_lanes = jnp.where(lane_match, pick(lane_hot.T, w_all.T, ((1,), (0,))).T, 0.0)
        w_rows = pick(tile_hot.T, w_lanes, ((1,), (0,)))
        for k in range(tiles):
            w_ref[k] = w_rows[k:k + 1]

    def met_weights():
        set_weights(chosen(packet_place(row_l, device_r), table_r, hot_at_r) * keep_lr
                    + (chosen(packet_place(row_r, device_l), table_l, hot_at_l) * keep_rl).T)

    if call == 0:
        met_weights()
    else:
        keep_ll = (blk_l <= blk_ll).astype(F32)
        eye = (lax.broadcasted_iota(jnp.int32, (gs, gs), 0) == lax.broadcasted_iota(jnp.int32, (gs, gs), 1))
        half_row = lax.broadcasted_iota(jnp.int32, (rs, rs), 0)
        half_col = lax.broadcasted_iota(jnp.int32, (rs, rs), 1)
        upper, lower = half_row < half_col, half_row > half_col

        @pl.when(jnp.logical_not(diag))
        def _():
            met_weights()
            w_ref[tiles] = jnp.zeros((1, LANES), F32)

        @pl.when(diag)
        def _():
            w_ll = chosen(packet_place(row_l, device_l), table_l, hot_at_l) * keep_ll
            w_sym = w_ll + w_ll.T
            set_weights(jnp.concatenate(
                [w_sym[:rs, rs:],
                 jnp.where(upper, w_sym[rs:, rs:], jnp.where(lower, w_sym[:rs, :rs], 0.0))], 0))
            self_l = jnp.sum(jnp.where(eye, w_ll, 0.0), 0, keepdims=True)
            w_ref[tiles] = jnp.concatenate([self_l, jnp.zeros((1, LANES - gs), F32)], 1)

    zeros = jnp.zeros((SUBS, LANES), F32)
    def image_rows(sl):
        a = [ref[:, sl].astype(F32) for ref in a_refs]
        if call == 0:
            b = [ref[:, sl].astype(F32) for ref in b_refs]
            left = jnp.where(swapped, jnp.concatenate(b, 0), jnp.concatenate(a, 0))
            right = jnp.where(swapped, a[0], b[1])
        else:
            left = jnp.concatenate(a, 0)
            right = jnp.where(diag, a[1], b_refs[0][:, sl].astype(F32))
        return jnp.concatenate([left, right, jnp.zeros((two - gs - rs, LANES), F32)], 0)

    def to_fields(x, store):
        t = jnp.concatenate([x, x], 0).T
        return [store(i, t[i * SUBS:(i + 1) * SUBS]) for i in range(per)]

    for blk in range(blocks):
        total = 0.0
        for ch in range(CHAN):
            x = image_rows(pl.ds(ch * npos + blk * LANES, LANES))
            x_ref[ch, :, pl.ds(blk * LANES, LANES)] = x
            total = total + x * x

        def store(i, t):
            j, v = col_of(blk * per + i)
            f_ref[0, j, v] = t
        to_fields(total * (1.0 / CHAN), store)
    for j in range(cols):
        for v in (0, side + 1):
            for l in range(LAYERS):
                v_ref[l, j, v] = zeros
                phi_ref[l, j, v] = zeros
            f_ref[0, j, v] = zeros
            f_ref[1, j, v] = zeros

    def block_of(ref_at, blk):
        vals = []
        for t in range(per):
            j, v = col_of(blk * per + t)
            vals.append(ref_at(j, v))
        return jnp.concatenate(vals, 0)

    inner = WEIGHT_VAR / (9.0 * 2.0 * math.pi)
    scales = [WEIGHT_VAR / (9.0 * CHAN)]
    while len(scales) < LAYERS:
        scales.append(scales[-1] * inner)

    def var_emit(l, scale):
        def emit(v, sums, extra):
            for j in range(cols):
                v_ref[l, j, v + 1] = sums[j] * (scale / scales[l]) + BIAS_VAR / scales[l]
            return extra
        return emit
    sweep(f_ref.at[0], side, cols, var_emit(0, WEIGHT_VAR / 9.0))
    for l in range(1, LAYERS):
        sweep(v_ref.at[l - 1], side, cols, var_emit(l, 0.5 * WEIGHT_VAR / 9.0 * scales[l - 1]))
    for l in range(LAYERS):
        for blk in range(blocks):
            t = block_of(lambda j, v: v_ref[l, j, v], blk).T[:two]
            sg_ref[l, :, pl.ds(blk * LANES, LANES)] = t * lax.rsqrt(t)
    totals = [zeros] * cols
    for j in range(cols):
        for v in range(side):
            totals[j] = totals[j] + v_ref[LAYERS - 1, j, v + 1]
    kself = jnp.sum(sum(totals), 0, keepdims=True) * (0.5 * WEIGHT_VAR / npos * scales[-1]) + BIAS_VAR

    def clear(i, _):
        sl = pl.ds(pl.multiple_of(i * LANES, LANES), LANES)
        d_ref[:, :, sl] = jnp.zeros((LAYERS + CHAN, two, LANES), F32)
        return 0
    lax.fori_loop(0, blocks, clear, 0)

    def pair_tile(k, _):
        a0 = pl.multiple_of(k * apt, SUBS)
        masked = jnp.logical_and(diag, a0 >= rs) if call == 1 else False
        lo0 = pl.multiple_of(jnp.maximum(a0 - rs, 0), SUBS)

        def put(blk, t):
            half = blk * per
            j = half // side
            v = half % side + 1
            for i in range(per):
                f_ref[0, j, v + i] = t[i * SUBS:(i + 1) * SUBS]

        def cross_plain(blk, _):
            sl = pl.ds(pl.multiple_of(blk * LANES, LANES), LANES)
            rows = []
            left = [x_ref[ch, pl.ds(a0, SUBS), sl] for ch in range(CHAN)]
            for b in range(rs):
                acc = left[0] * x_ref[0, gs + b:gs + b + 1, sl]
                for ch in range(1, CHAN):
                    acc = acc + left[ch] * x_ref[ch, gs + b:gs + b + 1, sl]
                rows.append(acc)
            put(blk, jnp.concatenate(rows, 0).T)
            return 0

        def cross_masked(blk, _):
            sl = pl.ds(pl.multiple_of(blk * LANES, LANES), LANES)
            rows = []
            left = [x_ref[ch, pl.ds(a0, SUBS), sl] for ch in range(CHAN)]
            low = [x_ref[ch, pl.ds(lo0, SUBS), sl] for ch in range(CHAN)]
            for b in range(rs):
                first = sub + lo0 < b
                acc = 0.0
                for ch in range(CHAN):
                    acc = acc + jnp.where(first, left[ch] * x_ref[ch, gs + b:gs + b + 1, sl],
                                          low[ch] * x_ref[ch, b:b + 1, sl])
                rows.append(acc)
            put(blk, jnp.concatenate(rows, 0).T)
            return 0

        def either(plain, with_mask):
            if call == 0:
                plain()
                return

            @pl.when(jnp.logical_not(masked))
            def _():
                plain()

            @pl.when(masked)
            def _():
                with_mask()

        either(lambda: lax.fori_loop(0, blocks, cross_plain, 0, unroll=True),
               lambda: lax.fori_loop(0, blocks, cross_masked, 0, unroll=True))

        ia, ib = lane % apt, lane // apt
        il, ir = ia + a0, ib + gs
        if call == 1:
            second = jnp.logical_and(masked, ib <= lo0 + ia)
            il = jnp.where(second, ia + lo0, il)
            ir = jnp.where(second, ib, ir)

        @pl.when(jnp.logical_or(k == 0, masked) if call == 1 else k == 0)
        def _():
            def gather(v, _):
                for l in range(LAYERS):
                    for j in range(cols):
                        kb_ref[l, j, v] = jnp.take_along_axis(v_ref[l, j, v + 1], ir, axis=1)
                return 0
            lax.fori_loop(0, side, gather, 0, unroll=True)

        parity = k % 2

        def relu_emit(l, dst):
            def emit(v, sums, extra):
                for j in range(cols):
                    k12 = sums[j] + BIAS_VAR / scales[l]
                    prod = jnp.take_along_axis(v_ref[l, j, v + 1], il, axis=1) * kb_ref[l, j, v]
                    inv = lax.rsqrt(prod)
                    cosine = k12 * inv
                    w = jnp.maximum(1.0 - jnp.abs(cosine), TINY)
                    poly = COEFFS[-1]
                    for c in COEFFS[-2::-1]:
                        poly = poly * w + c
                    angle = (w * lax.rsqrt(w)) * poly
                    phi = jnp.where(cosine >= 0.0, math.pi - angle, angle)
                    rest = jnp.maximum(prod - k12 * k12, TINY)
                    root = rest * lax.rsqrt(rest)
                    value = root + phi * k12
                    phi_ref[l, j, v + 1] = phi
                    sin_ref[parity, l, j, v + 1] = root * inv
                    if dst is None:
                        extra = extra + value
                    else:
                        f_ref[dst, j, v + 1] = value
                return extra
            return emit

        sweep(f_ref.at[0], side, cols, relu_emit(0, 1))
        sweep(f_ref.at[1], side, cols, relu_emit(1, 0))
        total = sweep(f_ref.at[0], side, cols, relu_emit(2, None), zeros)
        kv_ref[k] = jnp.sum(total, 0, keepdims=True) * (WEIGHT_VAR / (2.0 * math.pi * npos) * scales[-1]) + BIAS_VAR

        wrow = jnp.broadcast_to(w_ref[k] * (WEIGHT_VAR / npos), (SUBS, LANES))
        wscaled = wrow * inner

        def back_emit(l, dst, scaled):
            def emit(v, sums, extra):
                for j in range(cols):
                    grad = sums[j] * wscaled if scaled else sums[j]
                    sin_ref[parity, l, j, v + 1] = sin_ref[parity, l, j, v + 1] * grad
                    f_ref[dst, j, v + 1] = phi_ref[l, j, v + 1] * grad
                return extra
            return emit
        sweep(phi_ref.at[2], side, cols, back_emit(1, 0, True))
        sweep(f_ref.at[0], side, cols, back_emit(0, 1, False))

        def last_emit(v, sums, extra):
            for j in range(cols):
                sin_ref[parity, LAYERS, j, v + 1] = sums[j]
            return extra
        sweep(f_ref.at[1], side, cols, last_emit)

        starts = [pl.multiple_of(a0 - apt, SUBS), a0]
        lows = [pl.multiple_of(jnp.maximum(a0 - apt - rs, 0), SUBS), lo0]
        wrows = [jnp.broadcast_to(w_ref[jnp.maximum(k - 1, 0)] * (WEIGHT_VAR / npos), (SUBS, LANES)), wrow]

        def fold(is_masked):
            def body(blk, _):
                sl = pl.ds(pl.multiple_of(blk * LANES, LANES), LANES)
                half = blk * per
                j = half // side
                v = half % side + 1

                def turned(t, l):
                    rows = [sin_ref[t, l, j, v + i] for i in range(per)]
                    if l == LAYERS - 1:
                        rows = [row * wrows[t] for row in rows]
                    h = jnp.concatenate(rows, 0).T
                    return [h[b * SUBS:(b + 1) * SUBS] for b in range(rs)]

                for l in range(LAYERS + 1):
                    h = [turned(t, l) for t in range(2)]
                    terms = [(l, sg_ref, l)] if l < LAYERS else [(LAYERS + ch, x_ref, ch) for ch in range(CHAN)]
                    for slot, src, at in terms:
                        left = [src[at, pl.ds(start, SUBS), sl] for start in starts]
                        totals = [0.0, 0.0]
                        if is_masked:
                            for t in range(2):
                                i = sub + t * apt
                                low = src[at, pl.ds(lows[t], SUBS), sl]
                                low_total = 0.0
                                for b in range(rs):
                                    terms_b = []
                                    if b > t * apt:
                                        first = h[t][b] if b >= (t + 1) * apt else jnp.where(i < b, h[t][b], 0.0)
                                        totals[t] = totals[t] + first * src[at, gs + b:gs + b + 1, sl]
                                        terms_b.append(first * left[t])
                                    if b < (t + 1) * apt - 1:
                                        other = h[t][b] if b < t * apt else jnp.where(i > b, h[t][b], 0.0)
                                        low_total = low_total + other * src[at, b:b + 1, sl]
                                        terms_b.append(other * low)
                                    r_ref[1 + t, slot, b, :, sl] = sum(terms_b)
                                at_rows = pl.ds(lows[t], SUBS)
                                d_ref[slot, at_rows, sl] = d_ref[slot, at_rows, sl] + low_total
                        else:
                            for b in range(rs):
                                right = src[at, gs + b:gs + b + 1, sl]
                                for t in range(2):
                                    totals[t] = totals[t] + h[t][b] * right
                                r_ref[k // 2, slot, b, :, sl] = h[0][b] * left[0] + h[1][b] * left[1]
                        for t in range(2):
                            at_rows = pl.ds(starts[t], SUBS)
                            d_ref[slot, at_rows, sl] = d_ref[slot, at_rows, sl] + totals[t]
                return 0
            lax.fori_loop(0, blocks, body, 0, unroll=True)

        @pl.when(parity == 1)
        def _():
            either(lambda: fold(False), lambda: fold(True))
        return 0

    lax.fori_loop(0, tiles, pair_tile, 0)

    def gather_right(within):
        def body(blk, _):
            sl = pl.ds(pl.multiple_of(blk * LANES, LANES), LANES)
            for slot in range(LAYERS + CHAN):
                for b0 in range(0, rs, SUBS):
                    sums = ([], [])
                    for b in range(b0, b0 + SUBS):
                        t = [r_ref[0, slot, b, :, sl], 0.0]
                        if not within:
                            t[0] = t[0] + r_ref[1, slot, b, :, sl]
                        for n in range(2 if within else 0):
                            part = r_ref[1 + n, slot, b, :, sl]
                            if n * apt <= b < (n + 1) * apt:
                                i = sub + n * apt
                                t[0] = t[0] + jnp.where(i < b, part, 0.0)
                                t[1] = t[1] + jnp.where(i > b, part, 0.0)
                            else:
                                low = int(b < n * apt)
                                t[low] = t[low] + part
                        sums[0].append(t[0])
                        sums[1].append(t[1])
                    for low in range(2 if within else 1):
                        at = pl.ds(b0 if low else gs + b0, SUBS)
                        d_ref[slot, at, sl] = d_ref[slot, at, sl] + fold_rows(sums[low])
            return 0
        lax.fori_loop(0, blocks, body, 0, unroll=True)

    if call == 0:
        gather_right(False)
    else:
        @pl.when(jnp.logical_not(diag))
        def _():
            gather_right(False)

        @pl.when(diag)
        def _():
            gather_right(True)

    selfw = w_ref[tiles] * (0.5 * WEIGHT_VAR / npos) if call == 1 else 0.0
    for l in range(LAYERS):
        dest = phi_ref if l == LAYERS - 1 else sin_ref.at[0]
        scale = (inner if l == 0 else 1.0) / (4.0 * math.pi)
        for blk in range(blocks):
            def store(i, t):
                j, v = col_of(blk * per + i)
                t = t * (lax.rsqrt(v_ref[l, j, v]) * scale)
                dest[l, j, v] = t + selfw if l == LAYERS - 1 else t
            to_fields(d_ref[l, :, pl.ds(blk * LANES, LANES)], store)

    def chain_emit(l):
        def emit(v, sums, extra):
            for j in range(cols):
                phi_ref[l, j, v + 1] = sin_ref[0, l, j, v + 1] + sums[j] * (0.5 * WEIGHT_VAR / 9.0)
            return extra
        return emit
    sweep(phi_ref.at[2], side, cols, chain_emit(1))
    sweep(phi_ref.at[1], side, cols, chain_emit(0))

    def final_emit(v, sums, extra):
        for j in range(cols):
            f_ref[0, j, v + 1] = sums[j] * (WEIGHT_VAR / 9.0 * 2.0 / CHAN)
        return extra
    sweep(phi_ref.at[0], side, cols, final_emit)
    for blk in range(blocks):
        e = block_of(lambda j, v: f_ref[0, j, v], blk).T[:two]
        at = pl.ds(blk * LANES, LANES)
        for ch in range(CHAN):
            sl = pl.ds(ch * npos + blk * LANES, LANES)
            grad = d_ref[LAYERS + ch, :, at] * (inner * inner / CHAN) + x_ref[ch, :, at] * e
            left, right = grad[:gs], grad[gs:gs + rs]
            if call == 0:
                near = jnp.where(swapped, right, left[:rs])
                gl_ref[:, sl] = jnp.concatenate([near, jnp.where(swapped, 0.0, left[rs:])], 0)
                gr_ref[:, sl] = jnp.where(swapped, left[rs:], right)
                rest_ref[:, sl] = jnp.where(swapped, left[:rs], 0.0)
            else:
                far = left[rs:] + jnp.where(diag, right, 0.0)
                gl_ref[:, sl] = jnp.concatenate([left[:rs], far], 0) + before_l_ref[:, sl]
                gr_ref[:, sl] = jnp.where(diag, before_r_ref[:, sl], right)

    kv = jnp.concatenate([kv_ref[k] for k in range(tiles)], 0)
    values = pick(lane_hot, jnp.where(lane_match, pick(tile_hot, kv, ((1,), (0,))), 0.0).T, ((1,), (0,))).T

    def spread(rows, vals, columns):
        placed = pick(columns.T, vals.T, ((1,), (0,))).T
        return pick(one_hot(rows, total_rows).T, placed, ((1,), (0,)))
    if call == 0:
        in_l = spread(table_place(row_r, device_l), values.T * keep_rl, hot_at_l)
        in_r = spread(table_place(row_l, device_r), values * keep_lr, hot_at_r)
        ours = pack_table(jnp.where(swapped, in_r, in_l))
        theirs = pack_table(jnp.where(swapped, in_l, in_r))
        gl_ref[:, feat:] = ours
        gr_ref[:, feat:] = jnp.concatenate([theirs[rs:], theirs[:rs]], 1)
    else:
        @pl.when(jnp.logical_not(diag))
        def _():
            in_l = spread(table_place(row_r, device_l), values.T * keep_rl, hot_at_l)
            in_r = spread(table_place(row_l, device_r), values * keep_lr, hot_at_r)
            theirs = pack_table(in_r)
            gl_ref[:, feat:] = pack_table(in_l) + before_l_ref[:, feat:]
            gr_ref[:, feat:] = theirs[:rs]
            rest_ref[...] = theirs[rs:]

        @pl.when(diag)
        def _():
            across, within = values[:rs], values[rs:]
            low_part, high_part = jnp.where(lower, within, 0.0), jnp.where(upper, within, 0.0)
            val_ll = jnp.concatenate([jnp.concatenate([low_part + low_part.T, across], 1),
                                      jnp.concatenate([across.T, high_part + high_part.T], 1)], 0)
            val_ll = jnp.where(eye, kself[:, :gs], val_ll) * keep_ll
            ours = spread(table_place(row_l, device_l), val_ll, hot_at_l)
            gl_ref[:, feat:] = pack_table(ours) + before_l_ref[:, feat:]
            gr_ref[:, feat:] = jnp.zeros((rs, gr_ref.shape[1] - feat), F32)
            rest_ref[...] = jnp.zeros(rest_ref.shape, F32)


def pair_kernel(call, mode, packets, dims, before=()):
    gs, npos, side, col_count, per_row, part = dims
    cols = side // SUBS
    tiles = gs * gs // 2 // LANES
    terms = LAYERS + CHAN
    field = (cols, side + 2, SUBS, LANES)
    feat = CHAN * npos
    tile_rows = 2 * gs // per_row
    lines = 4 * tile_rows * per_row * tile_rows // (per_row * part)
    rs = gs // 2
    shapes = [(gs, feat + lines)] + ([(rs, feat + 2 * lines), (rs, feat)] if call == 0 else [(rs, feat + lines), (rs, lines)])
    vm = pl.BlockSpec(memory_space=pltpu.VMEM)
    operands = (mode, *packets, *before)
    return pl.pallas_call(
        functools.partial(kernel_body, dims, call),
        out_shape=[jax.ShapeDtypeStruct(shape, F32) for shape in shapes],
        in_specs=[pl.BlockSpec(memory_space=pltpu.SMEM)] + [vm] * (len(operands) - 1),
        out_specs=[vm] * len(shapes),
        scratch_shapes=[
            pltpu.VMEM((CHAN, 2 * gs, npos), F32),
            pltpu.VMEM((LAYERS,) + field, F32),
            pltpu.VMEM((LAYERS, cols, side, SUBS, LANES), F32),
            pltpu.VMEM((LAYERS, 2 * gs, npos), F32),
            pltpu.VMEM((2,) + field, F32),
            pltpu.VMEM((LAYERS,) + field, F32),
            pltpu.VMEM((2, LAYERS + 1) + field, F32),
            pltpu.VMEM((terms, 2 * gs, npos), F32),
            pltpu.VMEM((3, terms, rs, SUBS, npos), F32),
            pltpu.VMEM((tiles + 1, 1, LANES), F32),
            pltpu.VMEM((tiles, 1, LANES), F32),
        ],
        compiler_params=pltpu.CompilerParams(vmem_limit_bytes=40 * 1024 * 1024),
        cost_estimate=pl.CostEstimate(flops=2 * 10**10, bytes_accessed=5 * 10**7, transcendentals=10**6),
        name="pair_fields",
    )(*operands)


def exchange(x, rows, cols, target):
    perm = []
    for r in range(rows):
        for c in range(cols):
            tr, tc = target(r, c)
            perm.append((r * cols + c, tr * cols + tc))
    return lax.ppermute(x, ("row", "col"), perm)


def body(images, cotangent):
    rows = lax.axis_size("row")
    cols = lax.axis_size("col")
    row = lax.axis_index("row")
    col = lax.axis_index("col")
    per_row, _, part, feat = images.shape
    members = rows // 2
    groups = 2 * cols
    assert members == cols and members & (members - 1) == 0
    tile_rows = part * rows
    last = members // 2
    npos = feat // CHAN
    side = math.isqrt(npos)
    count = per_row * part
    gs = members * count
    own = images.reshape(count * CHAN, SUBS, npos // SUBS).transpose(0, 2, 1).reshape(count, feat)

    def partner_of(r, c, flip=0, turn=0):
        half, m = r // members, r % members
        step = m // last * (2 * m + 1 - members) + (1 - m // last) * (2 * m + 2)
        other = (half * cols + c + step) % groups
        return (other // cols ^ turn) * members + (m ^ flip), other % cols

    holders = {}
    for r in range(rows):
        for c in range(cols):
            holders[partner_of(r, c)] = (r, c)

    def holder_of(r, c, flip=0, turn=0):
        return holders[r ^ flip ^ turn * members, c]

    def swap(x, bit):
        return exchange(x, rows, cols, lambda r, c: (r ^ bit, c))

    cot_own = cotangent.reshape(count // 2, -1)
    packet = jnp.concatenate([own, jnp.concatenate([cot_own, swap(cot_own, members)], 0)], 1)
    bits = []
    while 1 << len(bits) < members:
        bits.append(1 << len(bits))
    near = packet
    for bit in bits[:-1]:
        near = jnp.concatenate([near, swap(near, bit)], 0)
    packets = [near, swap(near, last)]
    packets += [exchange(near, rows, cols, functools.partial(holder_of, flip=f)) for f in (0, last)]
    p_row, p_col = partner_of(row, col)
    member = row % members
    half = row // members
    flag = member == last - 1
    mode = jnp.stack([flag.astype(jnp.int32), member, col, half, p_col, p_row // members, row, p_row])
    mode = mode.astype(jnp.int32)

    dims = (gs, npos, side, cols, per_row, part)
    half_count = gs // 2
    gl, gr, rest = pair_kernel(0, mode, packets, dims)
    first = exchange(gr, rows, cols, partner_of)
    gl, gr, rest = pair_kernel(1, mode, packets, dims, before=(gl, rest))
    lines = rest.shape[1]
    gr = exchange(gr, rows, cols, partner_of)
    rest = exchange(rest, rows, cols, functools.partial(partner_of, flip=last))
    met = swap(gl[half_count:] + first[:, :feat + lines], last)
    out = gl[:half_count] + met + gr + jnp.pad(first[:, feat + lines:] + rest, ((0, 0), (feat, 0)))
    for bit in bits[-2::-1]:
        n = out.shape[0] // 2
        out = out[:n] + swap(out[n:], bit)
    table = out[:, feat:]
    n = lines // 2
    table = table[:, :n] + swap(table[:, n:], members)
    width = per_row * tile_rows
    table = table.reshape(count, n // width, width).transpose(1, 0, 2)
    grads = out[:, :feat].reshape(count * CHAN, npos // SUBS, SUBS).transpose(0, 2, 1)
    return (table.reshape(2, tile_rows, per_row, 1, tile_rows),
            grads.reshape(per_row, 1, part, feat))


def solution(mesh):
    return jax.shard_map(
        body,
        mesh=mesh,
        in_specs=(P(None, "col", "row", None), P("row", None, None, "col", None)),
        out_specs=(P("row", None, None, "col", None), P(None, "col", "row", None)),
        check_vma=False,
    )
```
